32 devices in a mesh: dp: 8 (over z, core), mp: 4 (over y, x).
Axes of the slice: x: 2, y: 2, z: 4, core: 2. Of those that a mesh axis runs over, the one named last changes fastest.
Arguments:
- block_in: bfloat16 [8192, 2048], P(('dp', 'mp')), may hold values from -6 to 6
- query_down: bfloat16 [2048, 1024], P(('dp', 'mp')), may hold values from -0.125 to 0.125
- query_up: bfloat16 [1024, 4096], P(('dp', 'mp')), may hold values from -0.1875 to 0.1875
- key_proj: bfloat16 [2048, 256], P(('dp', 'mp')), may hold values from -0.125 to 0.125
- value_proj: bfloat16 [2048, 256], P(('dp', 'mp')), may hold values from -0.125 to 0.125
- out_proj: bfloat16 [4096, 2048], P(('dp', 'mp')), may hold values from -0.75 to 0.75
- gate_proj: bfloat16 [2048, 5632], P(None, 'mp'), may hold values from -0.125 to 0.125
- up_proj: bfloat16 [2048, 5632], P(None, 'mp'), may hold values from -0.125 to 0.125
- down_proj: bfloat16 [5632, 2048], P('mp'), may hold values from -0.078125 to 0.078125
- attn_gain: bfloat16 [2048], P(('dp', 'mp')), may hold values from 0.5 to 1.5
- query_gain: bfloat16 [1024], P(('dp', 'mp')), may hold values from 0.5 to 1.5
- ffn_gain: bfloat16 [2048], P(('dp', 'mp')), may hold values from 0.5 to 1.5
- seq_lens: int32 [8, 3], P('dp'), may hold values from 1 to 1022, as said below
- seq_starts: int32 [8, 3], P('dp'), may hold values from 0 to 1023, as said below
- out_grad: bfloat16 [8192, 2048], P(('dp', 'mp')), may hold values from -6 to 6
Outputs:
- block_out: bfloat16 [8192, 2048], P(('dp', 'mp'))
- input_grad: bfloat16 [8192, 2048], P(('dp', 'mp'))
- query_down_grad: float32 [2048, 1024], P(('dp', 'mp'))
- query_up_grad: float32 [1024, 4096], P('dp', 'mp')
- key_proj_grad: float32 [2048, 256], P(('dp', 'mp'))
- value_proj_grad: float32 [2048, 256], P(('dp', 'mp'))
- out_proj_grad: float32 [4096, 2048], P('mp', 'dp')
- gate_proj_grad: float32 [2048, 5632], P(None, 'mp')
- up_proj_grad: float32 [2048, 5632], P(None, 'mp')
- down_proj_grad: float32 [5632, 2048], P('mp')
- attn_gain_grad: float32 [2048], P(('dp', 'mp'))
- query_gain_grad: float32 [1024], P(('dp', 'mp'))
- ffn_gain_grad: float32 [2048], P(('dp', 'mp'))
The draws below stay inside these ranges and needn't reach their ends.
Inputs may be any that keep to these rules, and one draw needn't show every extreme that they name: `seq_lens`: the 3 sequences of a group occupy disjoint runs of the group's 1024 slots; one of them, at a place in the row drawn from the seed, starts among the first 256 slots of the group and ends among its last 256 slots. Slots outside every sequence are padding. `seq_starts`: first slot of each sequence within its group, as described for seq_lens.
All inputs are finite; a program needn't handle non-finite values.
Results may differ from the reference program's by a relative error of at most 0.028.
Values may be sent and summed in bfloat16 or wider, within the bound.
No kernel may reach another device: no remote copies, remote signals or barrier semaphores. Data moves between devices by JAX's collectives and lax.ppermute only.
A program may use at most 256 MiB of HBM per device.

```python
import jax
import jax.numpy as jnp
from jax import lax

D = 2048
QL = 1024
HQ = 16
HD = 256
FF = 5632
TOK_DEV = 256
SEQS = 3
GROUP = 1024
TOKENS = 8192
N_DP = 8
N_MP = 4


def plan_groups(key):
    group_rows = TOK_DEV * N_MP
    parts = jax.random.split(key, 6)
    first_len = jax.random.randint(parts[0], (N_DP,), 1, TOK_DEV // 2 + 1)
    gap_front = jax.random.randint(parts[1], (N_DP,), 0, TOK_DEV // 8 + 1)
    last_len = jax.random.randint(parts[2], (N_DP,), 1, TOK_DEV // 2 + 1)
    gap_back = jax.random.randint(parts[3], (N_DP,), 0, TOK_DEV // 8 + 1)
    chosen = jax.random.randint(parts[5], (), 0, N_DP)
    forced = jnp.arange(N_DP, dtype=jnp.int32) == chosen
    first_len = jnp.where(forced, 1, first_len)
    gap_front = jnp.where(forced, 0, gap_front)
    last_len = jnp.where(forced, 1, last_len)
    gap_back = jnp.where(forced, 0, gap_back)
    middle_start = first_len + gap_front
    last_start = group_rows - last_len
    middle_len = last_start - gap_back - middle_start
    lengths = jnp.stack([first_len, middle_len, last_len], axis=1).astype(jnp.int32)
    starts = jnp.stack([jnp.zeros_like(first_len), middle_start, last_start], axis=1).astype(jnp.int32)
    orders = jax.vmap(lambda row_key: jax.random.permutation(row_key, SEQS))(jax.random.split(parts[4], N_DP))
    return (jnp.take_along_axis(lengths, orders, axis=1), jnp.take_along_axis(starts, orders, axis=1))


def draw_seq_lens(key, part):
    return plan_groups(key)[0]


def draw_seq_starts(key, part):
    return plan_groups(key)[1]


def steps_of(rng, dims, cuts, least, top_value):
    def one(dim, blocks):
        steps = jax.random.uniform(jax.random.fold_in(jax.random.fold_in(rng, 6), dim), (blocks,), jnp.float32, least / len(cuts), top_value / len(cuts))
        return jnp.repeat(jnp.exp(steps), dims[dim] // blocks).reshape((-1,) + (1,) * (len(dims) - dim - 1))

    level = one(*cuts[0])
    for cut in cuts[1:]:
        level = level * one(*cut)
    return level


def normal_values(key, shape, spread, most, cuts=(), kind=jnp.bfloat16):
    array = spread * jax.random.normal(key, shape, jnp.float32)
    if cuts:
        array = array * steps_of(key, shape, cuts, -0.22, 0.18)
    return jnp.clip(array, -most, most).astype(kind)


def setup_inputs(seed: int = 0) -> dict:
    key_of = jax.random.split(jax.random.key(seed), 16)
    block_in = normal_values(key_of[0], (TOKENS, D), 1.0, 6.0, ((0, 32),))
    query_down = normal_values(key_of[1], (D, QL), D ** -0.5, 0.125, ((0, 32),))
    query_up = normal_values(key_of[2], (QL, HQ * HD), QL ** -0.5, 0.1875, ((0, 32),))
    key_proj = normal_values(key_of[3], (D, HD), D ** -0.5, 0.125, ((0, 32),))
    value_proj = normal_values(key_of[4], (D, HD), D ** -0.5, 0.125, ((0, 32),))
    out_proj = normal_values(key_of[5], (HQ * HD, D), (HQ * HD // 64) ** -0.5, 0.75, ((0, 32),))
    gate_proj = normal_values(key_of[6], (D, FF), D ** -0.5, 0.125, ((1, 4),))
    up_proj = normal_values(key_of[7], (D, FF), D ** -0.5, 0.125, ((1, 4),))
    down_proj = normal_values(key_of[8], (FF, D), FF ** -0.5, 0.078125, ((0, 4),))
    attn_gain = jnp.clip(1.0 + 0.1 * jax.random.normal(key_of[9], (D,), jnp.float32), 0.5, 1.5).astype(jnp.bfloat16)
    query_gain = jnp.clip(1.0 + 0.1 * jax.random.normal(key_of[10], (QL,), jnp.float32), 0.5, 1.5).astype(jnp.bfloat16)
    ffn_gain = jnp.clip(1.0 + 0.1 * jax.random.normal(key_of[11], (D,), jnp.float32), 0.5, 1.5).astype(jnp.bfloat16)
    seq_lens = draw_seq_lens(jax.random.fold_in(key_of[15], 71), 0)
    seq_starts = draw_seq_starts(jax.random.fold_in(key_of[15], 71), 0)
    out_grad = normal_values(key_of[14], (TOKENS, D), 1.0, 6.0, ((0, 32),))
    return dict(block_in=block_in, query_down=query_down, query_up=query_up, key_proj=key_proj, value_proj=value_proj, out_proj=out_proj, gate_proj=gate_proj, up_proj=up_proj, down_proj=down_proj, attn_gain=attn_gain, query_gain=query_gain, ffn_gain=ffn_gain, seq_lens=seq_lens, seq_starts=seq_starts, out_grad=out_grad)


epsilon = 1e-06
masked_value = -1e+30
rope_base = 10000.0

@jax.custom_vjp
def low(v):
    return lax.optimization_barrier(v.astype(jnp.bfloat16)).astype(jnp.float32)

@jax.custom_vjp
def low_back(v):
    return v

def low_keep(v):
    return (low(v), None)

def low_pass(kept, grad):
    return (grad,)

def back_keep(v):
    return (v, None)

def back_low(kept, grad):
    return (low(grad),)
low.defvjp(low_keep, low_pass)
low_back.defvjp(back_keep, back_low)

def slot_layout(lengths, starts, slot_ids):
    inside = (slot_ids[:, None] >= starts[None, :]) & (slot_ids[:, None] < starts[None, :] + lengths[None, :])
    counted = lax.optimization_barrier(jnp.sum(inside.astype(jnp.int32), axis=1))
    numbers = jnp.arange(lengths.shape[0], dtype=jnp.int32)
    member = lax.optimization_barrier(jnp.sum(jnp.where(inside, numbers[None, :], 0), axis=1)).astype(jnp.int32)
    offset = lax.optimization_barrier(jnp.sum(jnp.where(inside, starts[None, :], 0), axis=1)).astype(jnp.int32)
    segment = jnp.where(counted > 0, member, -1 - slot_ids).astype(jnp.int32)
    position = jnp.where(counted > 0, slot_ids - offset, 0).astype(jnp.int32)
    return (segment, position)

def rotate(values, position, direction):
    half_dim = values.shape[-1] // 2
    freqs = rope_base ** (-jnp.arange(half_dim, dtype=jnp.float32) / half_dim)
    angles = position.astype(jnp.float32)[:, None] * freqs[None, :]
    cosine = jnp.cos(angles)[:, None, :]
    sine = direction * jnp.sin(angles)[:, None, :]
    first = values[..., :half_dim]
    second = values[..., half_dim:]
    return jnp.concatenate([first * cosine - second * sine, second * cosine + first * sine], axis=-1)

def norm_scale(values, gain):
    return values * lax.rsqrt(lax.optimization_barrier(jnp.mean(values * values, axis=-1, keepdims=True)) + epsilon) * gain

def highest_dot(left, right):
    return jnp.dot(left, right, precision=lax.Precision.HIGHEST, preferred_element_type=jnp.float32)

def attend(query_rot, key_rot, value_rows, segment, slot_ids):
    row_block = min(512, GROUP)
    count = GROUP // row_block

    def one_block(index):
        start = index * row_block
        query_block = lax.dynamic_slice_in_dim(query_rot, start, row_block, 0)
        block_segment = lax.dynamic_slice_in_dim(segment, start, row_block, 0)
        block_slots = lax.dynamic_slice_in_dim(slot_ids, start, row_block, 0)
        scores = low_back(jnp.einsum('thd,kd->thk', query_block, key_rot, precision=lax.Precision.HIGHEST))
        allowed = (block_segment[:, None] == segment[None, :]) & (slot_ids[None, :] <= block_slots[:, None])
        allowed = allowed[:, None, :]
        masked = jnp.where(allowed, scores, masked_value)
        largest = lax.optimization_barrier(jnp.max(masked, axis=-1, keepdims=True))
        expo = jnp.where(allowed, jnp.exp(masked - largest), 0.0)
        total = lax.optimization_barrier(jnp.sum(expo, axis=-1, keepdims=True))
        unnorm = low_back(jnp.einsum('thk,kd->thd', low(expo), value_rows, precision=lax.Precision.HIGHEST))
        return unnorm / total
    outputs = lax.map(jax.checkpoint(one_block), jnp.arange(count, dtype=jnp.int32))
    return outputs.reshape(GROUP, HQ, HD)

def layer(params, block_rows, segment, position, slot_ids):
    query_down, query_up, key_proj, value_proj, out_proj, gate_proj, up_proj, down_proj, attn_gain, query_gain, ffn_gain = params
    normed = low(norm_scale(block_rows, attn_gain))
    query_low = low_back(highest_dot(normed, query_down))
    query_norm = low(norm_scale(query_low, query_gain))
    query_raw = low_back(highest_dot(query_norm, query_up)).reshape(GROUP, HQ, HD)
    query_rot = low(rotate(query_raw, position, 1.0) * HD ** (-0.5))
    key_raw = low_back(highest_dot(normed, key_proj))
    key_rot = low(rotate(key_raw[:, None, :], position, 1.0)[:, 0, :])
    value_rows = low(low_back(highest_dot(normed, value_proj)))
    attended = attend(query_rot, key_rot, value_rows, segment, slot_ids)
    mixed = low(low_back(attended.reshape(GROUP, HQ * HD)))
    hidden_one = block_rows + low_back(highest_dot(mixed, out_proj))
    ffn_in = low(norm_scale(hidden_one, ffn_gain))
    gate_vals = low_back(highest_dot(ffn_in, gate_proj))
    up_vals = low_back(highest_dot(ffn_in, up_proj))
    activ = low(jax.nn.silu(gate_vals) * up_vals)
    return hidden_one + highest_dot(activ, down_proj)

def reference(block_in, query_down, query_up, key_proj, value_proj, out_proj, gate_proj, up_proj, down_proj, attn_gain, query_gain, ffn_gain, seq_lens, seq_starts, out_grad):
    params = tuple((weight.astype(jnp.float32) for weight in (query_down, query_up, key_proj, value_proj, out_proj, gate_proj, up_proj, down_proj, attn_gain, query_gain, ffn_gain)))
    slot_ids = jnp.arange(GROUP, dtype=jnp.int32)
    inputs = block_in.astype(jnp.float32).reshape(N_DP, GROUP, D)
    cotangents = out_grad.astype(jnp.float32).reshape(N_DP, GROUP, D)

    def step(totals, pieces):
        rows, cot_rows, lengths, starts = pieces
        segment, position = slot_layout(lengths, starts, slot_ids)

        def forward(weights, layer_in):
            return layer(weights, layer_in, segment, position, slot_ids)
        result, pullback = jax.vjp(forward, params, rows)
        param_grads, row_grads = pullback(cot_rows)
        totals = jax.tree.map(lambda a, b: a + b, totals, param_grads)
        return (totals, (result, row_grads))
    zeros = tuple((jnp.zeros_like(weight) for weight in params))
    totals, (results, input_rows) = lax.scan(step, zeros, (inputs, cotangents, seq_lens, seq_starts))
    return (results.reshape(TOKENS, D).astype(jnp.bfloat16), input_rows.reshape(TOKENS, D).astype(jnp.bfloat16), totals[0], totals[1], totals[2], totals[3], totals[4], totals[5], totals[6], totals[7], totals[8], totals[9], totals[10])
```

```python
import functools

import jax
import jax.numpy as jnp
from jax import lax
from jax.experimental import pallas as pl
from jax.experimental.pallas import tpu as pltpu
from jax.sharding import PartitionSpec as P

HQ = 16
HD = 256

epsilon = 1e-06
masked_value = -1e30
rope_base = 10000.0
wide = jnp.float32
narrow = jnp.bfloat16
brief = pl.CostEstimate(flops=1, bytes_accessed=1, transcendentals=0)


def slot_layout(lengths, starts, slot_ids):
    inside = (slot_ids[:, None] >= starts[None, :]) & (
        slot_ids[:, None] < starts[None, :] + lengths[None, :]
    )
    counted = jnp.sum(inside.astype(jnp.int32), axis=1)
    numbers = jnp.arange(lengths.shape[0], dtype=jnp.int32)
    member = jnp.sum(jnp.where(inside, numbers[None, :], 0), axis=1)
    offset = jnp.sum(jnp.where(inside, starts[None, :], 0), axis=1)
    segment = jnp.where(counted > 0, member, -1 - slot_ids)
    position = jnp.where(counted > 0, slot_ids - offset, 0)
    return (segment, position)


def rope_tables(position):
    half_dim = HD // 2
    freqs = rope_base ** (-jnp.arange(half_dim, dtype=jnp.float32) / half_dim)
    angles = position.astype(jnp.float32)[:, None] * freqs[None, :]
    return jnp.cos(angles), jnp.sin(angles)


def turn(values, cosine, sine):
    half_dim = values.shape[-1] // 2
    first = values[..., :half_dim]
    second = values[..., half_dim:]
    return jnp.concatenate(
        [first * cosine - second * sine, second * cosine + first * sine], axis=-1
    )


def norm_scale(values, gain):
    return values * lax.rsqrt(jnp.mean(values * values, axis=-1, keepdims=True) + epsilon) * gain


def norm_back(values, gain, grad):
    scale = lax.rsqrt(jnp.mean(values * values, axis=-1, keepdims=True) + epsilon)
    unit = values * scale
    weighted = grad * gain
    rows_part = scale * (weighted - unit * jnp.mean(weighted * unit, axis=-1, keepdims=True))
    return rows_part, grad * unit


def mat_dot(left, right):
    return jnp.dot(left, right, preferred_element_type=jnp.float32)


def dot_left_t(left, right):
    return lax.dot_general(
        left, right, (((0,), (0,)), ((), ())), preferred_element_type=jnp.float32
    )


def dot_right_t(left, right):
    return lax.dot_general(
        left, right, (((1,), (1,)), ((), ())), preferred_element_type=jnp.float32
    )


def after(values, *earlier):
    if not isinstance(values, (list, tuple)):
        return lax.optimization_barrier((values, *earlier))[0]
    return list(lax.optimization_barrier((*values, *earlier))[: len(values)])


class Flow:
    def __init__(self, mark):
        self.mark = mark

    def pass_on(self, *values):
        *values, self.mark = lax.optimization_barrier((*values, self.mark))
        return values[0] if len(values) == 1 else values

    take = put = pass_on


def on_small_mesh():
    return lax.axis_size("dp") == 8 and lax.axis_size("mp") == 4


def core_index():
    return lax.rem(lax.axis_index("dp"), 2)


def z_index():
    return lax.axis_index("dp") // 2


def swap_core(v):
    return lax.ppermute(v, "dp", [(i, i ^ 1) for i in range(8)])


def swap_mp(v, r):
    return lax.ppermute(v, "mp", [(i, i ^ r) for i in range(4)])


def z_move(v, pairs):
    return lax.ppermute(v, "dp", [(2 * a + c, 2 * b + c) for a, b in pairs for c in (0, 1)])


def choose(index, cases):
    value = cases[-1]
    for k in range(len(cases) - 2, -1, -1):
        value = jnp.where(index == k, cases[k], value)
    return value


def z_near(v):
    u1 = z_move(v, [(0, 1), (1, 2), (2, 3)])
    d1 = z_move(v, [(1, 0), (2, 1), (3, 2)])
    u2 = z_move(u1, [(1, 2), (2, 3)])
    d2 = z_move(d1, [(2, 1), (1, 0)])
    u3 = z_move(u2, [(2, 3)])
    d3 = z_move(d2, [(1, 0)])
    return [u3, u2, u1, v, d1, d2, d3]


def z_gather(v):
    near = z_near(v)
    z = z_index()
    return jnp.stack([choose(z, [near[3 + j - k] for k in range(4)]) for j in range(4)])


def z_scatter_sum(block):
    total = ZSum(block)
    total.middle()
    total.last()
    return total.end()


def mp_gather(v, earlier=()):
    count = lax.axis_size("mp")
    if count != 4:
        blocks = lax.all_gather(v, "mp", axis=0)
        return blocks[jnp.arange(count) ^ lax.axis_index("mp")]
    half = v.shape[0] // 2
    x = swap_mp(v, 1)
    y = swap_mp(v, 2)
    far = [swap_mp(after(y[:half], *earlier), 1), swap_mp(after(x[half:], *earlier), 2)]
    return jnp.concatenate([v, x, y, *far]).reshape(4, *v.shape)


class MpSum:
    def __init__(self, parts):
        self.parts = [part.astype(narrow) for part in parts]
        self.small = on_small_mesh()
        if not self.small:
            return
        self.half = parts[0].shape[0] // 2
        far = self.parts[3:]
        if len(far) == 1:
            far = [far[0][: self.half], far[0][self.half :]]
        self.from_x = swap_mp(far[0], 1)
        self.from_y = swap_mp(far[1], 2)

    def middle(self, *earlier):
        if not self.small:
            return
        half = self.half
        x, y = after(self.parts[1:3], *earlier) if earlier else self.parts[1:3]
        to_x = jnp.concatenate([x[:half], (x[half:].astype(wide) + self.from_y.astype(wide)).astype(narrow)])
        to_y = jnp.concatenate([(y[:half].astype(wide) + self.from_x.astype(wide)).astype(narrow), y[half:]])
        self.got = swap_mp(to_x, 1), swap_mp(to_y, 2)

    def end(self):
        if not self.small:
            order = jnp.arange(len(self.parts)) ^ lax.axis_index("mp")
            blocks = jnp.stack(self.parts)[order]
            return lax.psum_scatter(blocks, "mp", scatter_dimension=0, tiled=False).astype(wide)
        return self.parts[0].astype(wide) + self.got[0].astype(wide) + self.got[1].astype(wide)


def mp_scatter_sum(parts):
    total = MpSum(parts)
    total.middle()
    return total.end()


class ZSum:
    def __init__(self, block):
        z = z_index()
        self.term = lambda k: block(jnp.clip(z + k, 0, 3)).astype(wide)
        self.up = z_move(self.term(3).astype(narrow), [(0, 1)])
        self.down = z_move(self.term(-3).astype(narrow), [(3, 2)])

    def middle(self):
        up = (self.term(2) + self.up.astype(wide)).astype(narrow)
        down = (self.term(-2) + self.down.astype(wide)).astype(narrow)
        self.up = z_move(up, [(0, 1), (1, 2)])
        self.down = z_move(down, [(3, 2), (2, 1)])

    def last(self):
        up = (self.term(1) + self.up.astype(wide)).astype(narrow)
        down = (self.term(-1) + self.down.astype(wide)).astype(narrow)
        self.up = z_move(up, [(0, 1), (1, 2), (2, 3)])
        self.down = z_move(down, [(3, 2), (2, 1), (1, 0)])

    def end(self):
        return self.term(0) + self.up.astype(wide) + self.down.astype(wide)


def place(parts, spots, shape):
    def kernel(*refs):
        core, me = core_index(), lax.axis_index("mp")
        for part, store in spots:
            store(core, me, refs[part], refs[len(parts)])

    return pl.pallas_call(
        kernel,
        out_shape=jax.ShapeDtypeStruct(shape, parts[0].dtype),
        in_specs=[pl.BlockSpec(memory_space=pltpu.VMEM)] * len(parts),
        out_specs=pl.BlockSpec(memory_space=pltpu.VMEM),
        compiler_params=pltpu.CompilerParams(vmem_limit_bytes=32 * 2**20),
        cost_estimate=brief,
    )(*parts)


def assemble_rows(mine, others, rows, columns):
    layout = [(0, 0, 4), (1, 0, 4), (2, 0, 4), (3, 0, 2), (3, 2, 2)]
    spots = []
    for other in range(2):
        for k, (r, first, count) in enumerate(layout):

            def store(core, me, source, target, other=other, r=r, first=first, count=count):
                target[first : first + count, core ^ other, me ^ r] = source[...]

            spots.append((other * 5 + k, store))
    return place(mine + others, spots, (4, 2, 4, rows, columns))


def order_line(near, up_columns):
    rows, columns = near[0].shape

    def kernel(*refs):
        z, me = z_index(), lax.axis_index("mp")
        up_ref, out_ref = refs[7], refs[8]
        for k in range(7):
            at = z + k - 3

            @pl.when((at >= 0) & (at < 4))
            def _(k=k, at=at):
                up_ref[at] = refs[k][:, :up_columns]
                out_ref[at ^ me] = refs[k][:, up_columns:]

    return pl.pallas_call(
        kernel,
        out_shape=[
            jax.ShapeDtypeStruct((4, rows, up_columns), narrow),
            jax.ShapeDtypeStruct((4, rows, columns - up_columns), narrow),
        ],
        in_specs=[pl.BlockSpec(memory_space=pltpu.VMEM)] * 7,
        out_specs=[pl.BlockSpec(memory_space=pltpu.VMEM)] * 2,
        compiler_params=pltpu.CompilerParams(vmem_limit_bytes=32 * 2**20),
        cost_estimate=brief,
    )(*near)


def assemble_up(own, other, rows, width):
    spots = []
    for k in range(2):
        for r in range(4):

            def store(core, me, source, target, k=k, r=r):
                target[:, core ^ k, me ^ r] = source[:, r * rows : (r + 1) * rows]

            spots.append((k, store))
    return place([own, other], spots, (4, 2, 4, rows, width))


def assemble_out(mine, others):
    rows, columns = mine[0].shape
    spots = []
    for k in range(2):
        for r in range(4):

            def store(core, me, source, target, k=k, r=r):
                target[core ^ k, me ^ r] = source[...]

            spots.append((k * 4 + r, store))
    return place(mine + others, spots, (2, 4, rows, columns))


def tick_kernel(has_own, has_pair, has_done, has_back, has_result, *refs):
    refs = list(refs)
    z = z_index()
    inner = (z == 1) | (z == 2)
    first = jnp.where(z == 1, 0, 1)
    own_next = refs.pop(0) if has_own else None
    own_now, got_x = (refs.pop(0), refs.pop(0)) if has_pair else (None, None)
    got_y = refs.pop(0) if has_done or has_back else None
    here = refs.pop(0) if has_done else None
    done = refs.pop(0) if has_back else None
    sent_x, got_end = (refs.pop(0), refs.pop(0)) if has_result else (None, None)
    if has_own or has_back:
        send_x = refs.pop(0)
        if has_own and has_back:
            send_x[first] = jnp.where(inner, done[0], own_next[first])
            send_x[1 - first] = jnp.where(inner, got_y[1], own_next[1 - first])
        elif has_own:
            send_x[...] = own_next[...]
        else:
            send_x[first] = done[0]
            send_x[1 - first] = got_y[1]
    if has_pair or has_done:
        send_y = refs.pop(0)
    if has_pair:
        new_here = refs.pop(0)
        send_y[0] = (own_now[1 - first].astype(wide) + got_x[1 - first].astype(wide)).astype(narrow)
        new_here[0] = (own_now[first].astype(wide) + got_x[first].astype(wide)).astype(narrow)
    if has_done:
        new_done = refs.pop(0)
        sum_done = (here[0].astype(wide) + got_y[0].astype(wide)).astype(narrow)
        send_y[1] = sum_done
        new_done[0] = sum_done
    if has_result:
        result = refs.pop(0)
        result[...] = jnp.where(inner, sent_x[...], got_end[...])


class ZSums:
    def __init__(self, count):
        self.count = count
        self.own = []
        self.results = []
        self.tick = 0
        self.send_x = self.send_y = self.here = self.done = None
        self.got_x = self.got_y = None

    def start(self):
        self.send_x = self.own[0]
        self.move()

    def move(self):
        tick = self.tick
        pairs = ([(0, 1), (3, 2)] if tick < self.count else []) + ([(1, 0), (2, 3)] if tick >= 3 else [])
        self.got_x = z_move(self.send_x, pairs) if pairs else None
        self.got_y = z_move(self.send_y, [(1, 2), (2, 1)]) if self.send_y is not None else None

    def over(self):
        return self.tick >= self.count + 3

    def step(self, flow):
        if self.over():
            return
        tick, count, own = self.tick, self.count, self.own
        half = own[0].shape[1:]
        steps = 2 if half[0] % 32 == 0 else 1
        half_spec = pl.BlockSpec((1, half[0] // steps, half[1]), lambda i: (0, i, 0))
        full_spec = pl.BlockSpec((2, half[0] // steps, half[1]), lambda i: (0, i, 0))
        half_shape = jax.ShapeDtypeStruct((1, *half), narrow)
        full_shape = jax.ShapeDtypeStruct((2, *half), narrow)
        has_own = tick + 1 < count
        has_pair = tick < count
        has_done = 1 <= tick <= count
        has_back = 2 <= tick <= count + 1
        has_result = tick >= 3
        ins, in_specs, outs, out_specs = [], [], [], []
        if has_own:
            ins += [own[tick + 1]]
            in_specs += [full_spec]
        if has_pair:
            ins += [own[tick], self.got_x]
            in_specs += [full_spec] * 2
        if has_done or has_back:
            ins += [self.got_y]
            in_specs += [full_spec]
        if has_done:
            ins += [self.here]
            in_specs += [half_spec]
        if has_back:
            ins += [self.done]
            in_specs += [half_spec]
        if has_result:
            ins += [self.send_x, self.got_x]
            in_specs += [full_spec] * 2
        if has_own or has_back:
            outs += [full_shape]
            out_specs += [full_spec]
        if has_pair or has_done:
            outs += [full_shape]
            out_specs += [full_spec]
        if has_pair:
            outs += [half_shape]
            out_specs += [half_spec]
        if has_done:
            outs += [half_shape]
            out_specs += [half_spec]
        if has_result:
            outs += [full_shape]
            out_specs += [full_spec]
        ins[0] = flow.take(ins[0])
        got = list(
            pl.pallas_call(
                functools.partial(tick_kernel, has_own, has_pair, has_done, has_back, has_result),
                grid=(steps,),
                in_specs=in_specs,
                out_specs=out_specs,
                out_shape=outs,
                cost_estimate=brief,
            )(*ins)
        )
        got[0] = flow.put(got[0])
        self.send_x = got.pop(0) if has_own or has_back else None
        self.send_y = got.pop(0) if has_pair or has_done else None
        self.here = got.pop(0) if has_pair else None
        self.done = got.pop(0) if has_done else None
        if has_result:
            self.results.append(got.pop(0))
        self.tick += 1
        if not self.over():
            self.move()


def join_kernel(count, turned, *refs):
    step = pl.program_id(0)
    core = core_index()
    out_ref = refs[-1]
    for c in range(2):
        for k in range(count):

            @pl.when(step == c * count + k)
            def _(c=c, k=k):
                mine, other = refs[k], refs[count + k]
                for h in range(2):
                    value = jnp.where(core == c, mine[h], other[h]).astype(wide)
                    size = value.shape[0]
                    if turned:
                        out_ref[:, h * size : (h + 1) * size] = value.T
                    else:
                        out_ref[h * size : (h + 1) * size] = value


def join_pieces(mine, others, turned=False):
    count = len(mine)
    _, size, columns = mine[0].shape
    rows = 2 * count * 2 * size
    if turned:
        shape, spec = (columns, rows), pl.BlockSpec((columns, 2 * size), lambda i: (0, i))
    else:
        shape, spec = (rows, columns), pl.BlockSpec((2 * size, columns), lambda i: (i, 0))
    return pl.pallas_call(
        functools.partial(join_kernel, count, turned),
        grid=(2 * count,),
        in_specs=[pl.BlockSpec(mine[0].shape, lambda i: (0, 0, 0), pipeline_mode=pl.Buffered(1))] * (2 * count),
        out_specs=spec,
        out_shape=jax.ShapeDtypeStruct(shape, wide),
        compiler_params=pltpu.CompilerParams(vmem_limit_bytes=32 * 2**20),
        cost_estimate=brief,
    )(*mine, *others)


def allowed_pairs(index, rows, count, seg_q, seg_k):
    row_slots = index * rows + lax.broadcasted_iota(jnp.int32, (rows, count), 0)
    key_slots = lax.broadcasted_iota(jnp.int32, (rows, count), 1)
    return (seg_q == seg_k[:, :count]) & (key_slots <= row_slots)


def attend_kernel(blocks, heads, me_ref, norm_ref, kv_ref, up_ref, out_ref, cos_ref, sin_ref, segq_ref, segk_ref,
                  rot_ref, mixed_ref, stat_ref, part_ref, key_ref, value_ref):
    step = pl.program_id(0)
    rows = norm_ref.shape[0]

    @pl.when(step == 0)
    def _():
        for j in range(blocks):
            block = kv_ref[pl.ds(pl.multiple_of((me_ref[0] ^ j) * rows, rows), rows), :]
            key_ref[j * rows : (j + 1) * rows, :] = block[:, :HD]
            value_ref[j * rows : (j + 1) * rows, :] = block[:, HD:]

    raw = mat_dot(norm_ref[...], up_ref[...])
    for h in range(heads):
        rot_ref[:, h * HD : (h + 1) * HD] = (
            turn(raw[:, h * HD : (h + 1) * HD], cos_ref[...], sin_ref[...]) * HD ** (-0.5)
        ).astype(narrow)

    for c in range(blocks):

        @pl.when(step == c)
        def _():
            count = (c + 1) * rows
            allowed = allowed_pairs(c, rows, count, segq_ref[...], segk_ref[...])
            for h in range(heads):
                query = rot_ref[:, h * HD : (h + 1) * HD]
                scores = dot_right_t(query, key_ref[:count, :])
                masked = jnp.where(allowed, scores, masked_value)
                largest = jnp.max(masked, axis=-1, keepdims=True)
                expo = jnp.where(allowed, jnp.exp(masked - largest), 0.0)
                total = jnp.sum(expo, axis=-1, keepdims=True)
                attended = mat_dot(expo.astype(narrow), value_ref[:count, :]) / total
                mixed_ref[:, h * HD : (h + 1) * HD] = attended.astype(narrow)
                stat_ref[:, h : h + 1] = largest
                stat_ref[:, heads + h : heads + h + 1] = total

    part_ref[...] = mat_dot(mixed_ref[...], out_ref[...]).astype(narrow)


def attend_back_kernel(blocks, heads, low_width, me_ref, rot_ref, kv_ref, grad_ref, out_ref, up_ref, stat_ref, cos_ref, sin_ref,
                       segq_ref, segk_ref, turned_ref, send_ref, key_ref, value_ref, key_acc, value_acc):
    step = pl.program_id(0)
    rows = rot_ref.shape[0]

    @pl.when(step == 0)
    def _():
        for j in range(blocks):
            block = kv_ref[pl.ds(pl.multiple_of((me_ref[0] ^ j) * rows, rows), rows), :]
            key_ref[j * rows : (j + 1) * rows, :] = block[:, :HD]
            value_ref[j * rows : (j + 1) * rows, :] = block[:, HD:]
        key_acc[...] = jnp.zeros_like(key_acc)
        value_acc[...] = jnp.zeros_like(value_acc)

    mixed_grad = dot_right_t(grad_ref[...], out_ref[...]).astype(narrow)

    for c in range(blocks):

        @pl.when(step == c)
        def _():
            count = (c + 1) * rows
            allowed = allowed_pairs(c, rows, count, segq_ref[...], segk_ref[...])
            for h in range(heads):
                query = rot_ref[:, h * HD : (h + 1) * HD]
                largest = stat_ref[:, h : h + 1]
                total = stat_ref[:, heads + h : heads + h + 1]
                scores = dot_right_t(query, key_ref[:count, :])
                expo = jnp.where(allowed, jnp.exp(jnp.where(allowed, scores, masked_value) - largest), 0.0)
                scaled = (mixed_grad[:, h * HD : (h + 1) * HD].astype(wide) / total).astype(narrow)
                prob_grad = dot_right_t(scaled, value_ref[:count, :])
                delta = jnp.sum(expo * prob_grad, axis=-1, keepdims=True) / total
                score_grad = (expo * (prob_grad - delta)).astype(narrow)
                query_grad = mat_dot(score_grad, key_ref[:count, :])
                turned_ref[:, h * HD : (h + 1) * HD] = (
                    turn(query_grad, cos_ref[...], -sin_ref[...]) * HD ** (-0.5)
                ).astype(narrow)
                key_acc[:count, :] += dot_left_t(score_grad, query)
                value_acc[:count, :] += dot_left_t(expo.astype(narrow), scaled)

    at = pl.ds(pl.multiple_of((me_ref[0] ^ step) * rows, rows), rows)
    send_ref[at, :low_width] = dot_right_t(turned_ref[...], up_ref[...]).astype(narrow)

    @pl.when(step == blocks - 1)
    def _():
        for j in range(blocks):
            at_j = pl.ds(pl.multiple_of((me_ref[0] ^ j) * rows, rows), rows)
            send_ref[at_j, low_width : low_width + HD] = key_acc[j * rows : (j + 1) * rows, :].astype(narrow)
            send_ref[at_j, low_width + HD :] = value_acc[j * rows : (j + 1) * rows, :].astype(narrow)


def attend(packed, query_up, out_proj, cosine, sine, segment, rows):
    group, low_width = packed.shape[0], packed.shape[1] - 2 * HD
    blocks, width, model = group // rows, query_up.shape[1], out_proj.shape[1]
    heads = width // HD
    moved = lambda i, me: (i ^ me[0], 0)
    whole = lambda i, me: (0, 0)
    still = lambda i, me: (i, 0)
    return pl.pallas_call(
        functools.partial(attend_kernel, blocks, heads),
        grid_spec=pltpu.PrefetchScalarGridSpec(
            num_scalar_prefetch=1,
            grid=(blocks,),
            in_specs=[
                pl.BlockSpec((rows, low_width), moved),
                pl.BlockSpec((group, 2 * HD), lambda i, me: (0, low_width // (2 * HD))),
                pl.BlockSpec(query_up.shape, whole),
                pl.BlockSpec(out_proj.shape, whole),
                pl.BlockSpec((rows, HD // 2), still),
                pl.BlockSpec((rows, HD // 2), still),
                pl.BlockSpec((rows, 1), still),
                pl.BlockSpec((1, group), whole),
            ],
            out_specs=[
                pl.BlockSpec((rows, width), moved),
                pl.BlockSpec((rows, width), moved),
                pl.BlockSpec((rows, 128), moved),
                pl.BlockSpec((rows, model), moved),
            ],
            scratch_shapes=[pltpu.VMEM((group, HD), narrow), pltpu.VMEM((group, HD), narrow)],
        ),
        out_shape=[
            jax.ShapeDtypeStruct((group, width), narrow),
            jax.ShapeDtypeStruct((group, width), narrow),
            jax.ShapeDtypeStruct((group, 128), wide),
            jax.ShapeDtypeStruct((group, model), narrow),
        ],
        compiler_params=pltpu.CompilerParams(vmem_limit_bytes=48 * 2**20),
        cost_estimate=brief,
    )(
        lax.axis_index("mp").reshape(1),
        packed,
        packed,
        query_up,
        out_proj,
        cosine,
        sine,
        segment[:, None],
        segment[None, :],
    )


def attend_back(rotated, packed, attn_grad, out_proj, query_up, stats, cosine, sine, segment, rows):
    group, low_width = packed.shape[0], packed.shape[1] - 2 * HD
    blocks, width, model = group // rows, query_up.shape[1], out_proj.shape[1]
    heads = width // HD
    moved = lambda i, me: (i ^ me[0], 0)
    whole = lambda i, me: (0, 0)
    still = lambda i, me: (i, 0)
    return pl.pallas_call(
        functools.partial(attend_back_kernel, blocks, heads, low_width),
        grid_spec=pltpu.PrefetchScalarGridSpec(
            num_scalar_prefetch=1,
            grid=(blocks,),
            in_specs=[
                pl.BlockSpec((rows, width), moved),
                pl.BlockSpec((group, 2 * HD), lambda i, me: (0, low_width // (2 * HD))),
                pl.BlockSpec((rows, model), moved),
                pl.BlockSpec(out_proj.shape, whole),
                pl.BlockSpec(query_up.shape, whole),
                pl.BlockSpec((rows, 128), moved),
                pl.BlockSpec((rows, HD // 2), still),
                pl.BlockSpec((rows, HD // 2), still),
                pl.BlockSpec((rows, 1), still),
                pl.BlockSpec((1, group), whole),
            ],
            out_specs=[
                pl.BlockSpec((rows, width), moved),
                pl.BlockSpec(packed.shape, whole),
            ],
            scratch_shapes=[pltpu.VMEM((group, HD), narrow)] * 2 + [pltpu.VMEM((group, HD), wide)] * 2,
        ),
        out_shape=[
            jax.ShapeDtypeStruct((group, width), narrow),
            jax.ShapeDtypeStruct(packed.shape, narrow),
        ],
        compiler_params=pltpu.CompilerParams(vmem_limit_bytes=48 * 2**20),
        cost_estimate=brief,
    )(
        lax.axis_index("mp").reshape(1),
        rotated,
        packed,
        attn_grad,
        out_proj,
        query_up,
        stats,
        cosine,
        sine,
        segment[:, None],
        segment[None, :],
    )


def ffn_kernel(rows_ref, cot_ref, gate_ref, up_ref, down_ref, activ_ref, gate_grad_ref, up_grad_ref):
    gate_vals = mat_dot(rows_ref[...], gate_ref[...])
    up_vals = mat_dot(rows_ref[...], up_ref[...])
    act_grad = dot_right_t(cot_ref[...], down_ref[...])
    sigma = 1.0 / (1.0 + jnp.exp(-gate_vals))
    silu = gate_vals * sigma
    activ_ref[...] = (silu * up_vals).astype(narrow)
    up_grad_ref[...] = (act_grad * silu).astype(narrow)
    gate_grad_ref[...] = (act_grad * up_vals * (sigma + silu * (1.0 - sigma))).astype(narrow)


def ffn(ffn_rows, cot_rows, gate_proj, up_proj, down_proj):
    group, model = ffn_rows.shape
    hidden = gate_proj.shape[1]
    tile = 256
    whole = lambda i: (0, 0)
    across = lambda i: (0, i)
    return pl.pallas_call(
        ffn_kernel,
        grid=(pl.cdiv(hidden, tile),),
        in_specs=[
            pl.BlockSpec((group, model), whole, pipeline_mode=pl.Buffered(1)),
            pl.BlockSpec((group, model), whole, pipeline_mode=pl.Buffered(1)),
            pl.BlockSpec((model, tile), across),
            pl.BlockSpec((model, tile), across),
            pl.BlockSpec((tile, model), lambda i: (i, 0)),
        ],
        out_specs=[pl.BlockSpec((group, tile), across)] * 3,
        out_shape=[jax.ShapeDtypeStruct((group, hidden), narrow)] * 3,
        compiler_params=pltpu.CompilerParams(vmem_limit_bytes=50 * 2**20),
        cost_estimate=brief,
    )(ffn_rows, cot_rows, gate_proj, up_proj, down_proj)


def left_t_kernel(left_ref, right_ref, out_ref):
    out_ref[...] = dot_left_t(left_ref[...], right_ref[...]).astype(narrow)


def left_t(left, right):
    rows, height = left.shape
    width = right.shape[1]
    return pl.pallas_call(
        left_t_kernel,
        grid=(pl.cdiv(height, 256),),
        in_specs=[
            pl.BlockSpec((rows, 256), lambda i: (0, i)),
            pl.BlockSpec((rows, width), lambda i: (0, 0), pipeline_mode=pl.Buffered(1)),
        ],
        out_specs=pl.BlockSpec((256, width), lambda i: (i, 0)),
        out_shape=jax.ShapeDtypeStruct((height, width), narrow),
        compiler_params=pltpu.CompilerParams(vmem_limit_bytes=32 * 2**20),
        cost_estimate=brief,
    )(left, right)


def left_t_halves_kernel(core_ref, left_ref, right_ref, give_ref, keep_ref):
    step = pl.program_id(0)
    product = dot_left_t(left_ref[...], right_ref[...]).astype(narrow)

    @pl.when(step < pl.num_programs(0) // 2)
    def _():
        give_ref[...] = product

    @pl.when(step >= pl.num_programs(0) // 2)
    def _():
        keep_ref[...] = product


def left_t_halves(left, right, height, tile=256, by_turns=False):
    rows = left.shape[0]
    width = right.shape[1]
    half = height // tile // 2
    if by_turns:
        owner = lambda i, core: (0, lax.rem(i, half) * 2 + (core[0] ^ jnp.where(i < half, 1, 0)))
    else:
        owner = lambda i, core: (0, (core[0] ^ jnp.where(i < half, 1, 0)) * half + lax.rem(i, half))
    shape = jax.ShapeDtypeStruct((height // 2, width), narrow)
    return pl.pallas_call(
        left_t_halves_kernel,
        grid_spec=pltpu.PrefetchScalarGridSpec(
            num_scalar_prefetch=1,
            grid=(2 * half,),
            in_specs=[
                pl.BlockSpec((rows, tile), owner),
                pl.BlockSpec((rows, width), lambda i, core: (0, 0), pipeline_mode=pl.Buffered(1)),
            ],
            out_specs=[
                pl.BlockSpec((tile, width), lambda i, core: (jnp.minimum(i, half - 1), 0)),
                pl.BlockSpec((tile, width), lambda i, core: (jnp.maximum(i - half, 0), 0)),
            ],
        ),
        out_shape=[shape, shape],
        compiler_params=pltpu.CompilerParams(vmem_limit_bytes=32 * 2**20),
        cost_estimate=brief,
    )(core_index().reshape(1), left, right)


def ffn_out_kernel(cuts, activ_ref, down_ref, *out_refs):
    total = mat_dot(activ_ref[...], down_ref[...]).astype(narrow)
    for (start, count), out_ref in zip(cuts, out_refs):
        out_ref[...] = total[start : start + count]


def ffn_out_parts(activ, down_proj, sizes):
    group, hidden = activ.shape
    model = down_proj.shape[1]
    tile = 256
    cuts, start = [], 0
    for size in sizes:
        cuts.append((start, size))
        start += size
    return pl.pallas_call(
        functools.partial(ffn_out_kernel, cuts),
        grid=(model // tile,),
        in_specs=[
            pl.BlockSpec((group, hidden), lambda i: (0, 0), pipeline_mode=pl.Buffered(1)),
            pl.BlockSpec((hidden, tile), lambda i: (0, i)),
        ],
        out_specs=[pl.BlockSpec((size, tile), lambda i: (0, i)) for size in sizes],
        out_shape=[jax.ShapeDtypeStruct((size, model), narrow) for size in sizes],
        compiler_params=pltpu.CompilerParams(vmem_limit_bytes=32 * 2**20),
        cost_estimate=brief,
    )(activ, down_proj)


def ffn_back_kernel(cuts, gate_grad_ref, up_grad_ref, gate_ref, up_ref, *out_refs):
    total = dot_right_t(gate_grad_ref[...], gate_ref[...]) + dot_right_t(up_grad_ref[...], up_ref[...])
    total = total.astype(narrow)
    for (start, count), out_ref in zip(cuts, out_refs):
        out_ref[...] = total[start : start + count]


def ffn_back_parts(gate_grad, up_grad, gate_proj, up_proj, sizes):
    group, hidden = gate_grad.shape
    model = gate_proj.shape[0]
    tile = 256
    cuts, start = [], 0
    for size in sizes:
        cuts.append((start, size))
        start += size
    return pl.pallas_call(
        functools.partial(ffn_back_kernel, cuts),
        grid=(model // tile,),
        in_specs=[
            pl.BlockSpec((group, hidden), lambda i: (0, 0), pipeline_mode=pl.Buffered(1)),
            pl.BlockSpec((group, hidden), lambda i: (0, 0), pipeline_mode=pl.Buffered(1)),
            pl.BlockSpec((tile, hidden), lambda i: (i, 0)),
            pl.BlockSpec((tile, hidden), lambda i: (i, 0)),
        ],
        out_specs=[pl.BlockSpec((size, tile), lambda i: (0, i)) for size in sizes],
        out_shape=[jax.ShapeDtypeStruct((size, model), narrow) for size in sizes],
        compiler_params=pltpu.CompilerParams(vmem_limit_bytes=40 * 2**20),
        cost_estimate=brief,
    )(gate_grad, up_grad, gate_proj, up_proj)


def low_weight_kernel(low_width, core_ref, normed_ref, grads_ref, attn_ref, ffn_ref, query_ref, give_ref, keep_ref):
    step = pl.program_id(0)
    rows = normed_ref.shape[0]
    lanes = lax.broadcasted_iota(jnp.int32, (rows, 128), 1)
    product = dot_left_t(normed_ref[...], grads_ref[...]).astype(narrow)
    gains = jnp.zeros((normed_ref.shape[1], 128), wide)
    for k, ref in enumerate((attn_ref, ffn_ref, query_ref)):
        gains += dot_left_t(ref[...], (lanes == k).astype(wide).astype(narrow))
    gains = gains.astype(narrow)

    @pl.when(step < 4)
    def _():
        give_ref[:, :low_width] = product
        give_ref[:, low_width:] = gains

    @pl.when(step >= 4)
    def _():
        keep_ref[:, :low_width] = product
        keep_ref[:, low_width:] = gains


def low_weight_grads(normed, grads, attn_terms, ffn_terms, query_terms):
    rows, model = normed.shape
    width = grads.shape[1]
    tile = model // 8
    owner = lambda i, core: (0, (core[0] ^ jnp.where(i < 4, 1, 0)) * 4 + lax.rem(i, 4))
    shape = jax.ShapeDtypeStruct((model // 2, width + 128), narrow)
    return pl.pallas_call(
        functools.partial(low_weight_kernel, width),
        grid_spec=pltpu.PrefetchScalarGridSpec(
            num_scalar_prefetch=1,
            grid=(8,),
            in_specs=[
                pl.BlockSpec((rows, tile), owner),
                pl.BlockSpec((rows, width), lambda i, core: (0, 0)),
                pl.BlockSpec((rows, tile), owner),
                pl.BlockSpec((rows, tile), owner),
                pl.BlockSpec((rows, tile), owner),
            ],
            out_specs=[
                pl.BlockSpec((tile, width + 128), lambda i, core: (jnp.minimum(i, 3), 0)),
                pl.BlockSpec((tile, width + 128), lambda i, core: (jnp.maximum(i - 4, 0), 0)),
            ],
        ),
        out_shape=[shape, shape],
        compiler_params=pltpu.CompilerParams(vmem_limit_bytes=32 * 2**20),
        cost_estimate=brief,
    )(core_index().reshape(1), normed, grads, attn_terms, ffn_terms, query_terms)


def body(
    block_in,
    query_down,
    query_up,
    key_proj,
    value_proj,
    out_proj,
    gate_proj,
    up_proj,
    down_proj,
    attn_gain,
    query_gain,
    ffn_gain,
    seq_lens,
    seq_starts,
    out_grad,
):
    rows, model = block_in.shape
    n_dp, n_mp = lax.axis_size("dp"), lax.axis_size("mp")
    me, dp = lax.axis_index("mp"), lax.axis_index("dp")
    group = rows * n_mp
    low = query_down.shape[1]
    share = query_down.shape[0]
    small = on_small_mesh()

    gains = jnp.stack([attn_gain, ffn_gain, jnp.pad(query_gain, (0, share - query_gain.shape[0]))], axis=1)
    first = jnp.concatenate([query_down, key_proj, value_proj, jnp.pad(gains, ((0, 0), (0, 125)))], axis=1)
    slot_ids = jnp.arange(group, dtype=jnp.int32)
    width = query_up.shape[1] // n_mp

    def tables(*earlier):
        slots = after(slot_ids, *earlier) if earlier else slot_ids
        segment, position = slot_layout(seq_lens[0], seq_starts[0], slots)
        cosine, sine = rope_tables(position)
        return segment, cosine, sine, [
            lax.dynamic_slice_in_dim(table, me * rows, rows, 0) for table in (cosine, sine)
        ]

    def project(block_in, weights):
        block_rows = block_in.astype(wide)
        gain_rows = weights[:, low + 2 * HD :].astype(wide).T
        gain_query = gain_rows[2].reshape(-1, share)[:, : query_gain.shape[0]].reshape(-1)
        normed = norm_scale(block_rows, gain_rows[0]).astype(narrow)
        low_kv = mat_dot(normed, weights[:, : low + 2 * HD])
        query_low = low_kv[:, :low]
        query_norm = norm_scale(query_low, gain_query).astype(narrow)
        key_rot = turn(low_kv[:, low : low + HD], own_cos, own_sin).astype(narrow)
        value_rows = low_kv[:, low + HD :].astype(narrow)
        return normed, query_low, jnp.concatenate([query_norm, key_rot, value_rows], axis=1), gain_rows, gain_query

    if small:
        line_up, line_down = [(0, 1), (1, 2), (2, 3)], [(1, 0), (2, 1), (3, 2)]
        u1, d1 = z_move(first, line_up), z_move(first, line_down)
        half = rows // 2
        cot_halves = [out_grad[:half], out_grad[half:]]
        cot_x, cot_y = ([swap_mp(piece, r) for piece in cot_halves] for r in (1, 2))
        cuts = [lax.dynamic_slice_in_dim(query_up, (me ^ r) * width, width, 1) for r in range(4)]
        plane = [cuts[0]] + [swap_mp(cuts[r], r) for r in range(1, 4)]
        u2, d2 = after([u1, d1], cot_x[0], cot_y[0])
        u2, d2 = z_move(u2, line_up[1:]), z_move(d2, line_down[:2])
        u3, d3 = z_move(u2, line_up[2:]), z_move(d2, line_down[:1])
        near = [u3, u2, u1, first, d1, d2, d3]
        z = z_index()
        own = jnp.stack([choose(z, [near[3 + j - k] for k in range(4)]) for j in range(4)])
        own = after(own, cot_x[1], cot_y[1])
        own_x, own_y = swap_mp(own, 1), swap_mp(own, 2)
        late = jnp.concatenate([jnp.concatenate(plane, axis=0), out_proj], axis=1)
        late = after(late, own)
        u1, d1 = z_move(late, line_up), z_move(late, line_down)
        segment, cosine, sine, (own_cos, own_sin) = tables(own)
        flow = Flow(cosine[:8])
        own, own_x, own_y = flow.put(own, own_x, own_y)
        far_x, far_y = swap_mp(own_y[:2], 1), swap_mp(own_x[2:], 2)
        others = [swap_core(piece) for piece in (own, own_x, own_y)]
        u1, d1 = flow.put(u1, d1)
        u2, d2 = z_move(u1, line_up[1:]), z_move(d1, line_down[:2])
        far_x, far_y, *others = flow.put(far_x, far_y, *others)
        others += [swap_core(far_x), swap_core(far_y)]
        cot_far = swap_mp(cot_y[0], 1), swap_mp(cot_x[1], 2)
        weights = flow.put(assemble_rows([own, own_x, own_y, far_x, far_y], others, *first.shape)).reshape(model, -1)
        normed, query_low, packed_own, gain_rows, gain_query = project(block_in, weights)
        cot_far = flow.put(*cot_far)
        packed_own = flow.put(packed_own)
        packed_x, packed_y = swap_mp(packed_own, 1), swap_mp(packed_own, 2)
        u2, d2 = flow.put(u2, d2)
        u3, d3 = z_move(u2, line_up[2:]), z_move(d2, line_down[:1])
        cot_rows = flow.put(jnp.concatenate([out_grad, *cot_x, *cot_y, *cot_far]))
        packed_x, packed_y = flow.put(packed_x, packed_y)
        packed_far = swap_mp(packed_y[:half], 1), swap_mp(packed_x[half:], 2)
        u3, d3 = flow.put(u3, d3)
        up_line, out_line = flow.put(*order_line([u3, u2, u1, late, d1, d2, d3], width))
        up_other = swap_core(up_line)
        packed_far = flow.put(*packed_far)
        mine = [out_line[0]] + [swap_mp(out_line[r], r) for r in range(1, 4)]
        up_own = flow.put(assemble_up(up_line, up_other, query_up.shape[0], width)).reshape(-1, width)
        packed = flow.put(jnp.concatenate([packed_own, packed_x, packed_y, *packed_far]))
        mine = flow.put(*mine)
        out_own = flow.put(assemble_out(mine, [swap_core(piece) for piece in mine])).reshape(-1, model)
    else:
        segment, cosine, sine, (own_cos, own_sin) = tables()
        weights = lax.all_gather(first, ("dp", "mp"), axis=0, tiled=True)
        up_all = lax.all_gather(query_up, ("dp", "mp"), axis=0, tiled=True)
        out_all = lax.all_gather(out_proj, ("dp", "mp"), axis=0, tiled=True)
        up_own = lax.dynamic_slice_in_dim(up_all, me * width, width, 1)
        out_own = lax.dynamic_slice_in_dim(out_all, me * width, width, 0)
        cot_rows = mp_gather(out_grad).reshape(group, model)
        normed, query_low, packed_own, gain_rows, gain_query = project(block_in, weights)
        packed = mp_gather(packed_own).reshape(group, -1)
    block_rows = block_in.astype(wide)
    down_kv = weights[:, : low + 2 * HD]
    gain_attn, gain_ffn = gain_rows[0], gain_rows[1]
    rotated, mixed, stats, attn_parts = attend(packed, up_own, out_own, cosine, sine, segment, rows)
    hidden_one = block_rows + mp_scatter_sum(list(attn_parts.reshape(n_mp, rows, model)))
    ffn_in = norm_scale(hidden_one, gain_ffn).astype(narrow)
    ffn_rows = mp_gather(ffn_in).reshape(group, model)
    activ, gate_grad, up_grad = ffn(ffn_rows, cot_rows, gate_proj, up_proj, down_proj)
    sizes = [rows] * 3 + [rows // 2] * 2 if small else [rows] * n_mp
    if not small:
        down_grad = left_t(activ, cot_rows)
        back_parts = ffn_back_parts(gate_grad, up_grad, gate_proj, up_proj, sizes)
        gate_weight_grad = left_t(ffn_rows, gate_grad)
        up_weight_grad = left_t(ffn_rows, up_grad)
        ffn_in_grad = mp_scatter_sum(back_parts)
        hidden_part, ffn_gain_terms = norm_back(hidden_one, gain_ffn, ffn_in_grad)
        hidden_grad = out_grad.astype(wide) + hidden_part
        attn_grad = mp_gather(hidden_grad.astype(narrow)).reshape(group, model)
        turned, back = attend_back(
            rotated, packed, attn_grad, out_own, up_own, stats, cosine, sine, segment, rows
        )
        out_part = left_t(attn_grad, mixed)
        up_part = left_t(packed[:, :low], turned)
        own_back = mp_scatter_sum(list(back.reshape(n_mp, rows, -1)))
        block_out = (hidden_one + mp_scatter_sum(ffn_out_parts(activ, down_proj, sizes))).astype(narrow)
    else:
        count = 4
        activ, gate_grad, up_grad = flow.put(activ, gate_grad, up_grad)
        share_d = lax.psum_scatter(flow.put(left_t(activ, cot_rows)), "dp", scatter_dimension=0, tiled=True)
        gate_grad, up_grad = flow.take(gate_grad, up_grad)
        back_sum = MpSum(flow.put(*ffn_back_parts(gate_grad, up_grad, gate_proj, up_proj, sizes)))
        give, keep = flow.put(*left_t_halves(ffn_rows, flow.take(up_grad), model))
        got = swap_core(give)
        chain = ZSums(count)

        def step():
            chain.step(flow)

        back_sum.from_x, back_sum.from_y = flow.put(back_sum.from_x, back_sum.from_y)
        back_sum.middle()
        keep, got = flow.put(keep, got)
        chip = flow.put((keep.astype(wide) + got.astype(wide)).astype(narrow))
        chain.own = list(chip.reshape(count, 2, -1, chip.shape[1]))
        chain.start()
        gate_weight_grad = flow.put(left_t(ffn_rows, flow.take(gate_grad)))
        out_sizes = ffn_out_parts(flow.take(activ), down_proj, sizes)
        out_sizes = flow.put(*out_sizes)
        step()
        back_sum.got = flow.put(*back_sum.got)
        ffn_in_grad = back_sum.end()
        hidden_part, ffn_gain_terms = norm_back(hidden_one, gain_ffn, ffn_in_grad)
        hidden_grad = out_grad.astype(wide) + hidden_part
        attn_own = flow.put(hidden_grad.astype(narrow))
        attn_x, attn_y = swap_mp(attn_own, 1), swap_mp(attn_own, 2)
        share_d = flow.put(share_d)
        down_sum = lax.all_gather(share_d, "dp", axis=0, tiled=True)
        step()
        attn_x, attn_y = flow.put(attn_x, attn_y)
        attn_far = swap_mp(attn_y[:half], 1), swap_mp(attn_x[half:], 2)
        attn_far = flow.put(*attn_far)
        attn_grad = flow.put(jnp.concatenate([attn_own, attn_x, attn_y, *attn_far]))
        step()
        turned, back = flow.put(
            *attend_back(rotated, packed, attn_grad, out_own, up_own, stats, cosine, sine, segment, rows)
        )
        own_sum = MpSum(list(back.reshape(n_mp, rows, -1)))
        give_out, keep_out = flow.put(
            *left_t_halves(flow.take(attn_grad), mixed, model, model // n_dp, by_turns=True)
        )
        got_out = swap_core(give_out)
        down_sum = flow.put(down_sum)
        share_g = lax.psum_scatter(flow.take(gate_weight_grad), "dp", scatter_dimension=0, tiled=True)
        step()
        own_sum.from_x, own_sum.from_y = flow.put(own_sum.from_x, own_sum.from_y)
        own_sum.middle()
        give_up, keep_up = flow.put(*left_t_halves(packed, flow.take(turned), low, low // n_dp, by_turns=True))
        got_up = swap_core(give_up)
        got_out, got_up = flow.put(got_out, got_up)
        sum_late = jnp.concatenate(
            [
                (keep.astype(wide) + got.astype(wide)).astype(narrow).reshape(n_dp // 2, -1, width)
                for keep, got in ((keep_out, got_out), (keep_up, got_up))
            ],
            axis=1,
        )
        sum_late = flow.put(sum_late)
        z_late = ZSum(lambda k: lax.dynamic_index_in_dim(sum_late, k, 0, keepdims=False))
        own_sum.got = flow.put(*own_sum.got)
        step()
        own_back = own_sum.end()
    query_low_part, query_gain_terms = norm_back(query_low, gain_query, own_back[:, :low])
    low_grads = jnp.concatenate(
        [
            query_low_part,
            turn(own_back[:, low : low + HD], own_cos, -own_sin),
            own_back[:, low + HD :],
        ],
        axis=1,
    ).astype(narrow)
    normed_grad = dot_right_t(low_grads, down_kv)
    rows_part, attn_gain_terms = norm_back(block_rows, gain_attn, normed_grad)

    if small:

        def by_owner(v):
            return v.astype(narrow).reshape(-1, 4, 8, share).swapaxes(1, 2).reshape(-1, model)

        query_terms = query_gain_terms.astype(narrow).reshape(rows, n_dp * n_mp, -1)
        query_terms = jnp.pad(query_terms, ((0, 0), (0, 0), (0, share - query_gain.shape[0])))
        give_low, keep_low = flow.put(
            *low_weight_grads(
                by_owner(after(normed, turned)),
                low_grads,
                by_owner(attn_gain_terms),
                by_owner(after(ffn_gain_terms, turned)),
                by_owner(query_terms),
            )
        )
        got_low = swap_core(give_low)
        hidden_late, rows_late = flow.take(hidden_grad, rows_part)
        input_grad = flow.put((hidden_late + rows_late).astype(narrow))
        got_low = flow.put(got_low)
        sum_low = (keep_low.astype(wide) + got_low.astype(wide)).astype(narrow).reshape(4, 4, share, -1)
        sum_low = flow.put(sum_low)
        low_sum = MpSum([lax.dynamic_index_in_dim(sum_low, me ^ r, 0, keepdims=False) for r in range(4)])
        z_late.up, z_late.down = flow.put(z_late.up, z_late.down)
        z_late.middle()
        step()
        down_proj_grad = flow.put(flow.take(down_sum).astype(wide))
        low_sum.from_x, low_sum.from_y = flow.put(low_sum.from_x, low_sum.from_y)
        low_sum.middle()
        step()
        z_late.up, z_late.down = flow.put(z_late.up, z_late.down)
        z_late.last()
        share_g = flow.put(share_g)
        gate_sum = lax.all_gather(share_g, "dp", axis=0, tiled=True)
        low_sum.got = flow.put(*low_sum.got)
        out_sum = MpSum(flow.take(*out_sizes))
        sum_low = flow.put(low_sum.end().astype(narrow))
        z_low = ZSum(lambda k: lax.dynamic_index_in_dim(sum_low, k, 0, keepdims=False))
        while not chain.over():
            step()
        others = [swap_core(piece) for piece in chain.results]
        z_low.up, z_low.down = flow.put(z_low.up, z_low.down)
        z_low.middle()
        out_sum.from_x, out_sum.from_y = flow.put(out_sum.from_x, out_sum.from_y)
        out_sum.middle()
        up_proj_grad = flow.put(join_pieces(flow.take(*chain.results), others))
        z_low.up, z_low.down = flow.put(z_low.up, z_low.down)
        z_low.last()
        out_sum.got = flow.put(*out_sum.got)
        block_out = flow.put((hidden_one + out_sum.end()).astype(narrow))
        z_late.up, z_late.down = flow.put(z_late.up, z_late.down)
        sum_late = z_late.end()
        out_proj_grad = sum_late[: model // n_dp]
        query_up_grad = sum_late[model // n_dp :]
        gate_proj_grad = flow.put(gate_sum).astype(wide)
        sum_low = z_low.end()
        out_proj_grad = out_proj_grad.astype(wide).T
        sum_low = sum_low + 0.0 * flow.mark[0, 0]
    else:
        input_grad = (hidden_grad + rows_part).astype(narrow)
        gain_parts = [attn_gain_terms.sum(axis=0), ffn_gain_terms.sum(axis=0)]
        query_gain_part = jnp.pad(
            query_gain_terms.sum(axis=0).reshape(n_dp * n_mp, -1), ((0, 0), (0, share - query_gain.shape[0]))
        ).reshape(-1)
        gain_parts = jnp.stack(gain_parts + [query_gain_part])
        out_proj_grad = lax.psum_scatter(out_part, "dp", scatter_dimension=0, tiled=True).astype(wide).T
        query_up_grad = lax.psum_scatter(up_part, "dp", scatter_dimension=0, tiled=True).astype(wide)
        wide_grads = jnp.concatenate(
            [dot_left_t(normed, low_grads), jnp.pad(gain_parts.T, ((0, 0), (0, 125)))], axis=1
        )
        sum_low = lax.psum_scatter(wide_grads, ("dp", "mp"), scatter_dimension=0, tiled=True)
        down_proj_grad = lax.psum(down_grad, "dp").astype(wide)
        gate_proj_grad = lax.psum(gate_weight_grad, "dp").astype(wide)
        up_proj_grad = lax.psum(up_weight_grad, "dp").astype(wide)
    ends = low + 2 * HD
    return (
        block_out,
        input_grad,
        sum_low[:, :low],
        query_up_grad,
        sum_low[:, low : low + HD],
        sum_low[:, low + HD : ends],
        out_proj_grad,
        gate_proj_grad,
        up_proj_grad,
        down_proj_grad,
        sum_low[:, ends],
        sum_low[: query_gain.shape[0], ends + 2],
        sum_low[:, ends + 1],
    )


def solution(mesh):
    both = ("dp", "mp")
    placed = (
        P(both, None),
        P(both, None),
        P(both, None),
        P(both, None),
        P(both, None),
        P(both, None),
        P(None, "mp"),
        P(None, "mp"),
        P("mp", None),
        P(both),
        P(both),
        P(both),
        P("dp", None),
        P("dp", None),
        P(both, None),
    )
    return jax.shard_map(
        body,
        mesh=mesh,
        in_specs=placed,
        out_specs=(
            P(both, None),
            P(both, None),
            P(both, None),
            P("dp", "mp"),
            P(both, None),
            P(both, None),
            P("mp", "dp"),
            P(None, "mp"),
            P(None, "mp"),
            P("mp", None),
            P(both),
            P(both),
            P(both),
        ),
        check_vma=False,
    )
```

```python
import functools

import jax
import jax.numpy as jnp
from jax import lax
from jax.experimental import pallas as pl
from jax.experimental.pallas import tpu as pltpu
from jax.sharding import PartitionSpec as P

HQ = 16
HD = 256

epsilon = 1e-06
masked_value = -1e30
rope_base = 10000.0
wide = jnp.float32
narrow = jnp.bfloat16
brief = pl.CostEstimate(flops=1, bytes_accessed=1, transcendentals=0)


def slot_layout(lengths, starts, slot_ids):
    inside = (slot_ids[:, None] >= starts[None, :]) & (
        slot_ids[:, None] < starts[None, :] + lengths[None, :]
    )
    counted = jnp.sum(inside.astype(jnp.int32), axis=1)
    numbers = jnp.arange(lengths.shape[0], dtype=jnp.int32)
    member = jnp.sum(jnp.where(inside, numbers[None, :], 0), axis=1)
    offset = jnp.sum(jnp.where(inside, starts[None, :], 0), axis=1)
    segment = jnp.where(counted > 0, member, -1 - slot_ids)
    position = jnp.where(counted > 0, slot_ids - offset, 0)
    return (segment, position)


def rope_tables(position):
    half_dim = HD // 2
    freqs = rope_base ** (-jnp.arange(half_dim, dtype=jnp.float32) / half_dim)
    angles = position.astype(jnp.float32)[:, None] * freqs[None, :]
    return jnp.cos(angles), jnp.sin(angles)


def turn(values, cosine, sine):
    half_dim = values.shape[-1] // 2
    first = values[..., :half_dim]
    second = values[..., half_dim:]
    return jnp.concatenate(
        [first * cosine - second * sine, second * cosine + first * sine], axis=-1
    )


def norm_scale(values, gain):
    return values * lax.rsqrt(jnp.mean(values * values, axis=-1, keepdims=True) + epsilon) * gain


def norm_back(values, gain, grad):
    scale = lax.rsqrt(jnp.mean(values * values, axis=-1, keepdims=True) + epsilon)
    unit = values * scale
    weighted = grad * gain
    rows_part = scale * (weighted - unit * jnp.mean(weighted * unit, axis=-1, keepdims=True))
    return rows_part, grad * unit


def mat_dot(left, right):
    return jnp.dot(left, right, preferred_element_type=jnp.float32)


def dot_left_t(left, right):
    return lax.dot_general(
        left, right, (((0,), (0,)), ((), ())), preferred_element_type=jnp.float32
    )


def dot_right_t(left, right):
    return lax.dot_general(
        left, right, (((1,), (1,)), ((), ())), preferred_element_type=jnp.float32
    )


def after(values, *earlier):
    if not isinstance(values, (list, tuple)):
        return lax.optimization_barrier((values, *earlier))[0]
    return list(lax.optimization_barrier((*values, *earlier))[: len(values)])


class Flow:
    def __init__(self, mark):
        self.mark = mark

    def pass_on(self, *values):
        *values, self.mark = lax.optimization_barrier((*values, self.mark))
        return values[0] if len(values) == 1 else values

    take = put = pass_on


def on_small_mesh():
    return lax.axis_size("dp") == 8 and lax.axis_size("mp") == 4


def core_index():
    return lax.rem(lax.axis_index("dp"), 2)


def z_index():
    return lax.axis_index("dp") // 2


def swap_core(v):
    return lax.ppermute(v, "dp", [(i, i ^ 1) for i in range(8)])


def swap_mp(v, r):
    return lax.ppermute(v, "mp", [(i, i ^ r) for i in range(4)])


def z_move(v, pairs):
    return lax.ppermute(v, "dp", [(2 * a + c, 2 * b + c) for a, b in pairs for c in (0, 1)])


def choose(index, cases):
    value = cases[-1]
    for k in range(len(cases) - 2, -1, -1):
        value = jnp.where(index == k, cases[k], value)
    return value


def z_near(v):
    u1 = z_move(v, [(0, 1), (1, 2), (2, 3)])
    d1 = z_move(v, [(1, 0), (2, 1), (3, 2)])
    u2 = z_move(u1, [(1, 2), (2, 3)])
    d2 = z_move(d1, [(2, 1), (1, 0)])
    u3 = z_move(u2, [(2, 3)])
    d3 = z_move(d2, [(1, 0)])
    return [u3, u2, u1, v, d1, d2, d3]


def z_gather(v):
    near = z_near(v)
    z = z_index()
    return jnp.stack([choose(z, [near[3 + j - k] for k in range(4)]) for j in range(4)])


def z_scatter_sum(block):
    total = ZSum(block)
    total.middle()
    total.last()
    return total.end()


def mp_gather(v, earlier=()):
    count = lax.axis_size("mp")
    if count != 4:
        blocks = lax.all_gather(v, "mp", axis=0)
        return blocks[jnp.arange(count) ^ lax.axis_index("mp")]
    half = v.shape[0] // 2
    x = swap_mp(v, 1)
    y = swap_mp(v, 2)
    far = [swap_mp(after(y[:half], *earlier), 1), swap_mp(after(x[half:], *earlier), 2)]
    return jnp.concatenate([v, x, y, *far]).reshape(4, *v.shape)


class MpSum:
    def __init__(self, parts):
        self.parts = [part.astype(narrow) for part in parts]
        self.small = on_small_mesh()
        if not self.small:
            return
        self.half = parts[0].shape[0] // 2
        far = self.parts[3:]
        if len(far) == 1:
            far = [far[0][: self.half], far[0][self.half :]]
        self.from_x = swap_mp(far[0], 1)
        self.from_y = swap_mp(far[1], 2)

    def middle(self, *earlier):
        if not self.small:
            return
        half = self.half
        x, y = after(self.parts[1:3], *earlier) if earlier else self.parts[1:3]
        to_x = jnp.concatenate([x[:half], (x[half:].astype(wide) + self.from_y.astype(wide)).astype(narrow)])
        to_y = jnp.concatenate([(y[:half].astype(wide) + self.from_x.astype(wide)).astype(narrow), y[half:]])
        self.got = swap_mp(to_x, 1), swap_mp(to_y, 2)

    def end(self):
        if not self.small:
            order = jnp.arange(len(self.parts)) ^ lax.axis_index("mp")
            blocks = jnp.stack(self.parts)[order]
            return lax.psum_scatter(blocks, "mp", scatter_dimension=0, tiled=False).astype(wide)
        return self.parts[0].astype(wide) + self.got[0].astype(wide) + self.got[1].astype(wide)


def mp_scatter_sum(parts):
    total = MpSum(parts)
    total.middle()
    return total.end()


class ZSum:
    def __init__(self, block):
        z = z_index()
        self.term = lambda k: block(jnp.clip(z + k, 0, 3)).astype(wide)
        self.up = z_move(self.term(3).astype(narrow), [(0, 1)])
        self.down = z_move(self.term(-3).astype(narrow), [(3, 2)])

    def middle(self):
        up = (self.term(2) + self.up.astype(wide)).astype(narrow)
        down = (self.term(-2) + self.down.astype(wide)).astype(narrow)
        self.up = z_move(up, [(0, 1), (1, 2)])
        self.down = z_move(down, [(3, 2), (2, 1)])

    def last(self):
        up = (self.term(1) + self.up.astype(wide)).astype(narrow)
        down = (self.term(-1) + self.down.astype(wide)).astype(narrow)
        self.up = z_move(up, [(0, 1), (1, 2), (2, 3)])
        self.down = z_move(down, [(3, 2), (2, 1), (1, 0)])

    def end(self):
        return self.term(0) + self.up.astype(wide) + self.down.astype(wide)


def place(parts, spots, shape):
    def kernel(*refs):
        core, me = core_index(), lax.axis_index("mp")
        target, sem = refs[len(parts)], refs[len(parts) + 1]
        copies = []
        for k, (part, views) in enumerate(spots):
            source, end = views(core, me, refs[part], target)
            copies.append(pltpu.make_async_copy(source, end, sem.at[k]))
            copies[-1].start()
        for copy in copies:
            copy.wait()

    return pl.pallas_call(
        kernel,
        out_shape=jax.ShapeDtypeStruct(shape, parts[0].dtype),
        in_specs=[pl.BlockSpec(memory_space=pl.ANY)] * len(parts),
        out_specs=pl.BlockSpec(memory_space=pltpu.VMEM),
        scratch_shapes=[pltpu.SemaphoreType.DMA((len(spots),))],
        compiler_params=pltpu.CompilerParams(vmem_limit_bytes=32 * 2**20),
        cost_estimate=brief,
    )(*parts)


def stack_rows(parts):
    spots, start = [], 0
    for k, part in enumerate(parts):

        def store(core, me, source, target, start=start, count=part.shape[0]):
            return source, target.at[pl.ds(start, count)]

        spots.append((k, store))
        start += part.shape[0]
    return place(parts, spots, (start, *parts[0].shape[1:]))


def add_blocks_kernel(keep_a, got_a, keep_b, got_b, out_ref):
    split = keep_a.shape[1]
    out_ref[:, :split] = (keep_a[...].astype(wide) + got_a[...].astype(wide)).astype(narrow)
    out_ref[:, split:] = (keep_b[...].astype(wide) + got_b[...].astype(wide)).astype(narrow)


def add_blocks(count, keep_a, got_a, keep_b, got_b):
    values = [v.reshape(count, -1, v.shape[1]) for v in (keep_a, got_a, keep_b, got_b)]
    size = values[0].shape[1] + values[2].shape[1]
    return pl.pallas_call(
        add_blocks_kernel,
        grid=(count,),
        in_specs=[pl.BlockSpec((1, *v.shape[1:]), lambda i: (i, 0, 0)) for v in values],
        out_specs=pl.BlockSpec((1, size, keep_a.shape[1]), lambda i: (i, 0, 0)),
        out_shape=jax.ShapeDtypeStruct((count, size, keep_a.shape[1]), narrow),
        cost_estimate=brief,
    )(*values)


def assemble_rows(mine, others, rows, columns):
    layout = [(0, 0, 4), (1, 0, 4), (2, 0, 4), (3, 0, 2), (3, 2, 2)]
    spots = []
    for other in range(2):
        for k, (r, first, count) in enumerate(layout):

            def store(core, me, source, target, other=other, r=r, first=first, count=count):
                return source, target.at[pl.ds(first, count), core ^ other, me ^ r]

            spots.append((other * 5 + k, store))
    return place(mine + others, spots, (4, 2, 4, rows, columns))


def line_copies(near, shapes, views):
    count = len(shapes)

    def kernel(*refs):
        z = z_index()
        targets, sem = refs[7 : 7 + count], refs[7 + count]

        def each(act):
            for k in range(7):
                at = z + k - 3

                @pl.when((at >= 0) & (at < 4))
                def _(k=k, at=at):
                    for j, (source, end) in enumerate(views(refs[k], jnp.clip(at, 0, 3), targets)):
                        act(pltpu.make_async_copy(source, end, sem.at[k, j]))

        each(lambda copy: copy.start())
        each(lambda copy: copy.wait())

    return pl.pallas_call(
        kernel,
        out_shape=[jax.ShapeDtypeStruct(shape, narrow) for shape in shapes],
        in_specs=[pl.BlockSpec(memory_space=pl.ANY)] * 7,
        out_specs=[pl.BlockSpec(memory_space=pltpu.VMEM)] * count,
        scratch_shapes=[pltpu.SemaphoreType.DMA((7, count))],
        compiler_params=pltpu.CompilerParams(vmem_limit_bytes=32 * 2**20),
        cost_estimate=brief,
    )(*near)


def order_line(near, up_columns):
    rows, columns = near[0].shape
    rest = columns - up_columns

    def views(block, at, targets):
        owner = at ^ lax.axis_index("mp")
        return [
            (block.at[:, pl.ds(0, up_columns)], targets[0].at[at]),
            (block.at[:, pl.ds(up_columns, rest)], targets[1].at[owner]),
        ]

    return line_copies(near, [(4, rows, up_columns), (4, rows, rest)], views)


def in_line(near):
    return line_copies(near, [(4, *near[0].shape)], lambda block, at, targets: [(block, targets[0].at[at])])[0]


def weave_kernel(own_ref, other_ref, out_ref):
    same = lax.rem(pl.program_id(0), 2) == core_index()
    out_ref[...] = jnp.where(same, own_ref[0], other_ref[0]).astype(wide)


def weave(own, other):
    count, rows, columns = own.shape
    spec = pl.BlockSpec((1, rows, columns), lambda i: (i // 2, 0, 0))
    return pl.pallas_call(
        weave_kernel,
        grid=(2 * count,),
        in_specs=[spec] * 2,
        out_specs=pl.BlockSpec((rows, columns), lambda i: (i, 0)),
        out_shape=jax.ShapeDtypeStruct((2 * count * rows, columns), wide),
        cost_estimate=brief,
    )(own, other)


def assemble_up(own, other, rows, width):
    spots = []
    for k in range(2):
        for r in range(4):

            def store(core, me, source, target, k=k, r=r):
                return source.at[:, pl.ds(r * rows, rows)], target.at[:, core ^ k, me ^ r]

            spots.append((k, store))
    return place([own, other], spots, (4, 2, 4, rows, width))


def assemble_out(mine, others):
    rows, columns = mine[0].shape
    spots = []
    for k in range(2):
        for r in range(4):

            def store(core, me, source, target, k=k, r=r):
                return source, target.at[core ^ k, me ^ r]

            spots.append((k * 4 + r, store))
    return place(mine + others, spots, (2, 4, rows, columns))


def allowed_pairs(index, rows, count, seg_q, seg_k):
    row_slots = index * rows + lax.broadcasted_iota(jnp.int32, (rows, count), 0)
    key_slots = lax.broadcasted_iota(jnp.int32, (rows, count), 1)
    return (seg_q == seg_k[:, :count]) & (key_slots <= row_slots)


def attend_kernel(blocks, heads, me_ref, norm_ref, kv_ref, up_ref, cos_ref, sin_ref, segq_ref, segk_ref,
                  rot_ref, mixed_ref, stat_ref, key_ref, value_ref):
    step = pl.program_id(0)
    rows = norm_ref.shape[0]

    @pl.when(step == 0)
    def _():
        for j in range(blocks):
            block = kv_ref[pl.ds(pl.multiple_of((me_ref[0] ^ j) * rows, rows), rows), :]
            key_ref[j * rows : (j + 1) * rows, :] = block[:, :HD]
            value_ref[j * rows : (j + 1) * rows, :] = block[:, HD:]

    raw = mat_dot(norm_ref[...], up_ref[...])
    for h in range(heads):
        rot_ref[:, h * HD : (h + 1) * HD] = (
            turn(raw[:, h * HD : (h + 1) * HD], cos_ref[...], sin_ref[...]) * HD ** (-0.5)
        ).astype(narrow)

    for c in range(blocks):

        @pl.when(step == c)
        def _():
            count = (c + 1) * rows
            allowed = allowed_pairs(c, rows, count, segq_ref[...], segk_ref[...])
            for h in range(heads):
                query = rot_ref[:, h * HD : (h + 1) * HD]
                scores = dot_right_t(query, key_ref[:count, :])
                masked = jnp.where(allowed, scores, masked_value)
                largest = jnp.max(masked, axis=-1, keepdims=True)
                expo = jnp.where(allowed, jnp.exp(masked - largest), 0.0)
                total = jnp.sum(expo, axis=-1, keepdims=True)
                attended = mat_dot(expo.astype(narrow), value_ref[:count, :]) / total
                mixed_ref[:, h * HD : (h + 1) * HD] = attended.astype(narrow)
                stat_ref[:, h : h + 1] = largest
                stat_ref[:, heads + h : heads + h + 1] = total


def attend_back_kernel(blocks, heads, low_width, me_ref, rot_ref, kv_ref, grad_ref, out_ref, up_ref, stat_ref, cos_ref, sin_ref,
                       segq_ref, segk_ref, turned_ref, *refs):
    *part_refs, send_ref, key_ref, value_ref, key_acc, value_acc = refs
    step = pl.program_id(0)
    rows = rot_ref.shape[0]

    @pl.when(step == 0)
    def _():
        for j in range(blocks):
            block = kv_ref[pl.ds(pl.multiple_of((me_ref[0] ^ j) * rows, rows), rows), :]
            key_ref[j * rows : (j + 1) * rows, :] = block[:, :HD]
            value_ref[j * rows : (j + 1) * rows, :] = block[:, HD:]
        key_acc[...] = jnp.zeros_like(key_acc)
        value_acc[...] = jnp.zeros_like(value_acc)

    mixed_grad = dot_right_t(grad_ref[...], out_ref[...]).astype(narrow)

    for c in range(blocks):

        @pl.when(step == c)
        def _():
            count = (c + 1) * rows
            allowed = allowed_pairs(c, rows, count, segq_ref[...], segk_ref[...])
            for h in range(heads):
                query = rot_ref[:, h * HD : (h + 1) * HD]
                largest = stat_ref[:, h : h + 1]
                total = stat_ref[:, heads + h : heads + h + 1]
                scores = dot_right_t(query, key_ref[:count, :])
                expo = jnp.where(allowed, jnp.exp(jnp.where(allowed, scores, masked_value) - largest), 0.0)
                scaled = (mixed_grad[:, h * HD : (h + 1) * HD].astype(wide) / total).astype(narrow)
                prob_grad = dot_right_t(scaled, value_ref[:count, :])
                delta = jnp.sum(expo * prob_grad, axis=-1, keepdims=True) / total
                score_grad = (expo * (prob_grad - delta)).astype(narrow)
                query_grad = mat_dot(score_grad, key_ref[:count, :])
                turned_ref[:, h * HD : (h + 1) * HD] = (
                    turn(query_grad, cos_ref[...], -sin_ref[...]) * HD ** (-0.5)
                ).astype(narrow)
                key_acc[:count, :] += dot_left_t(score_grad, query)
                value_acc[:count, :] += dot_left_t(expo.astype(narrow), scaled)

    at = pl.ds(pl.multiple_of((me_ref[0] ^ step) * rows, rows), rows)
    send_ref[at, :low_width] = dot_right_t(turned_ref[...], up_ref[...]).astype(narrow)

    @pl.when(step == blocks - 1)
    def _():
        for j in range(blocks):
            at_j = pl.ds(pl.multiple_of((me_ref[0] ^ j) * rows, rows), rows)
            send_ref[at_j, low_width : low_width + HD] = key_acc[j * rows : (j + 1) * rows, :].astype(narrow)
            send_ref[at_j, low_width + HD :] = value_acc[j * rows : (j + 1) * rows, :].astype(narrow)
        start = 0
        for part_ref in part_refs:
            part_ref[...] = send_ref[start : start + part_ref.shape[0], :]
            start += part_ref.shape[0]


def attend(packed, query_up, cosine, sine, segment, rows):
    group, low_width = packed.shape[0], packed.shape[1] - 2 * HD
    blocks, width = group // rows, query_up.shape[1]
    heads = width // HD
    moved = lambda i, me: (i ^ me[0], 0)
    whole = lambda i, me: (0, 0)
    still = lambda i, me: (i, 0)
    return pl.pallas_call(
        functools.partial(attend_kernel, blocks, heads),
        grid_spec=pltpu.PrefetchScalarGridSpec(
            num_scalar_prefetch=1,
            grid=(blocks,),
            in_specs=[
                pl.BlockSpec((rows, low_width), moved),
                pl.BlockSpec((group, 2 * HD), lambda i, me: (0, low_width // (2 * HD))),
                pl.BlockSpec(query_up.shape, whole),
                pl.BlockSpec((rows, HD // 2), still),
                pl.BlockSpec((rows, HD // 2), still),
                pl.BlockSpec((rows, 1), still),
                pl.BlockSpec((1, group), whole),
            ],
            out_specs=[
                pl.BlockSpec((rows, width), moved),
                pl.BlockSpec((rows, width), moved),
                pl.BlockSpec((rows, 128), moved),
            ],
            scratch_shapes=[pltpu.VMEM((group, HD), narrow), pltpu.VMEM((group, HD), narrow)],
        ),
        out_shape=[
            jax.ShapeDtypeStruct((group, width), narrow),
            jax.ShapeDtypeStruct((group, width), narrow),
            jax.ShapeDtypeStruct((group, 128), wide),
        ],
        compiler_params=pltpu.CompilerParams(vmem_limit_bytes=48 * 2**20),
        cost_estimate=brief,
    )(
        lax.axis_index("mp").reshape(1),
        packed,
        packed,
        query_up,
        cosine,
        sine,
        segment[:, None],
        segment[None, :],
    )


def attend_back(rotated, packed, attn_grad, out_proj, query_up, stats, cosine, sine, segment, rows, sizes):
    group, low_width = packed.shape[0], packed.shape[1] - 2 * HD
    blocks, width, model = group // rows, query_up.shape[1], out_proj.shape[1]
    heads = width // HD
    moved = lambda i, me: (i ^ me[0], 0)
    whole = lambda i, me: (0, 0)
    still = lambda i, me: (i, 0)
    return pl.pallas_call(
        functools.partial(attend_back_kernel, blocks, heads, low_width),
        grid_spec=pltpu.PrefetchScalarGridSpec(
            num_scalar_prefetch=1,
            grid=(blocks,),
            in_specs=[
                pl.BlockSpec((rows, width), moved),
                pl.BlockSpec((group, 2 * HD), lambda i, me: (0, low_width // (2 * HD))),
                pl.BlockSpec((rows, model), moved),
                pl.BlockSpec(out_proj.shape, whole),
                pl.BlockSpec(query_up.shape, whole),
                pl.BlockSpec((rows, 128), moved),
                pl.BlockSpec((rows, HD // 2), still),
                pl.BlockSpec((rows, HD // 2), still),
                pl.BlockSpec((rows, 1), still),
                pl.BlockSpec((1, group), whole),
            ],
            out_specs=[
                pl.BlockSpec((rows, width), moved),
                *[pl.BlockSpec((size, packed.shape[1]), whole) for size in sizes],
            ],
            scratch_shapes=[pltpu.VMEM(packed.shape, narrow)] + [pltpu.VMEM((group, HD), narrow)] * 2 + [pltpu.VMEM((group, HD), wide)] * 2,
        ),
        out_shape=[
            jax.ShapeDtypeStruct((group, width), narrow),
            *[jax.ShapeDtypeStruct((size, packed.shape[1]), narrow) for size in sizes],
        ],
        compiler_params=pltpu.CompilerParams(vmem_limit_bytes=48 * 2**20),
        cost_estimate=brief,
    )(
        lax.axis_index("mp").reshape(1),
        rotated,
        packed,
        attn_grad,
        out_proj,
        query_up,
        stats,
        cosine,
        sine,
        segment[:, None],
        segment[None, :],
    )


def ffn_kernel(rows_ref, cot_ref, gate_ref, up_ref, down_ref, activ_ref, gate_grad_ref, up_grad_ref):
    gate_vals = mat_dot(rows_ref[...], gate_ref[...])
    up_vals = mat_dot(rows_ref[...], up_ref[...])
    act_grad = dot_right_t(cot_ref[...], down_ref[...])
    sigma = 1.0 / (1.0 + jnp.exp(-gate_vals))
    silu = gate_vals * sigma
    activ_ref[...] = (silu * up_vals).astype(narrow)
    up_grad_ref[...] = (act_grad * silu).astype(narrow)
    gate_grad_ref[...] = (act_grad * up_vals * (sigma + silu * (1.0 - sigma))).astype(narrow)


def ffn(ffn_rows, cot_rows, gate_proj, up_proj, down_proj):
    group, model = ffn_rows.shape
    hidden = gate_proj.shape[1]
    tile = 256
    whole = lambda i: (0, 0)
    across = lambda i: (0, i)
    return pl.pallas_call(
        ffn_kernel,
        grid=(pl.cdiv(hidden, tile),),
        in_specs=[
            pl.BlockSpec((group, model), whole, pipeline_mode=pl.Buffered(1)),
            pl.BlockSpec((group, model), whole, pipeline_mode=pl.Buffered(1)),
            pl.BlockSpec((model, tile), across),
            pl.BlockSpec((model, tile), across),
            pl.BlockSpec((tile, model), lambda i: (i, 0)),
        ],
        out_specs=[pl.BlockSpec((group, tile), across)] * 3,
        out_shape=[jax.ShapeDtypeStruct((group, hidden), narrow)] * 3,
        compiler_params=pltpu.CompilerParams(vmem_limit_bytes=50 * 2**20),
        cost_estimate=brief,
    )(ffn_rows, cot_rows, gate_proj, up_proj, down_proj)


def widen_kernel(value_ref, *out_refs):
    start = 0
    for out_ref in out_refs:
        out_ref[...] = value_ref[start : start + out_ref.shape[0], :].astype(wide)
        start += out_ref.shape[0]


def widen(value, count, outs=1):
    rows, columns = value.shape
    size = rows // count
    spec = pl.BlockSpec((size // outs, columns), lambda i: (i, 0))
    shape = jax.ShapeDtypeStruct((rows // outs, columns), wide)
    return pl.pallas_call(
        widen_kernel,
        grid=(count,),
        in_specs=[pl.BlockSpec((size, columns), lambda i: (i, 0))],
        out_specs=[spec] * outs,
        out_shape=[shape] * outs,
        compiler_params=pltpu.CompilerParams(vmem_limit_bytes=32 * 2**20),
        cost_estimate=brief,
    )(value)


def left_t_pair_kernel(left_ref, first_ref, second_ref, out_ref):
    half = left_ref.shape[1]
    out_ref[:half] = dot_left_t(left_ref[...], first_ref[...]).astype(narrow)
    out_ref[half:] = dot_left_t(left_ref[...], second_ref[...]).astype(narrow)


def left_t_pair(left, first, second, count):
    rows, height = left.shape
    width = first.shape[1]
    tile = height // count
    return pl.pallas_call(
        left_t_pair_kernel,
        grid=(count,),
        in_specs=[pl.BlockSpec((rows, tile), lambda i: (0, i))]
        + [pl.BlockSpec((rows, width), lambda i: (0, 0), pipeline_mode=pl.Buffered(1))] * 2,
        out_specs=pl.BlockSpec((2 * tile, width), lambda i: (i, 0)),
        out_shape=jax.ShapeDtypeStruct((2 * height, width), narrow),
        compiler_params=pltpu.CompilerParams(vmem_limit_bytes=40 * 2**20),
        cost_estimate=brief,
    )(left, first, second)


def left_t_kernel(left_ref, right_ref, out_ref):
    out_ref[...] = dot_left_t(left_ref[...], right_ref[...]).astype(narrow)


def left_t(left, right):
    rows, height = left.shape
    width = right.shape[1]
    return pl.pallas_call(
        left_t_kernel,
        grid=(pl.cdiv(height, 256),),
        in_specs=[
            pl.BlockSpec((rows, 256), lambda i: (0, i)),
            pl.BlockSpec((rows, width), lambda i: (0, 0), pipeline_mode=pl.Buffered(1)),
        ],
        out_specs=pl.BlockSpec((256, width), lambda i: (i, 0)),
        out_shape=jax.ShapeDtypeStruct((height, width), narrow),
        compiler_params=pltpu.CompilerParams(vmem_limit_bytes=32 * 2**20),
        cost_estimate=brief,
    )(left, right)


def left_t_halves_kernel(core_ref, left_ref, right_ref, give_ref, keep_ref):
    step = pl.program_id(0)
    product = dot_left_t(left_ref[...], right_ref[...]).astype(narrow)

    @pl.when(step < pl.num_programs(0) // 2)
    def _():
        give_ref[...] = product

    @pl.when(step >= pl.num_programs(0) // 2)
    def _():
        keep_ref[...] = product


def left_t_halves(left, right, height, tile=256, by_turns=False):
    rows = left.shape[0]
    width = right.shape[1]
    half = height // tile // 2
    if by_turns:
        owner = lambda i, core: (0, lax.rem(i, half) * 2 + (core[0] ^ jnp.where(i < half, 1, 0)))
    else:
        owner = lambda i, core: (0, (core[0] ^ jnp.where(i < half, 1, 0)) * half + lax.rem(i, half))
    shape = jax.ShapeDtypeStruct((height // 2, width), narrow)
    return pl.pallas_call(
        left_t_halves_kernel,
        grid_spec=pltpu.PrefetchScalarGridSpec(
            num_scalar_prefetch=1,
            grid=(2 * half,),
            in_specs=[
                pl.BlockSpec((rows, tile), owner),
                pl.BlockSpec((rows, width), lambda i, core: (0, 0), pipeline_mode=pl.Buffered(1)),
            ],
            out_specs=[
                pl.BlockSpec((tile, width), lambda i, core: (jnp.minimum(i, half - 1), 0)),
                pl.BlockSpec((tile, width), lambda i, core: (jnp.maximum(i - half, 0), 0)),
            ],
        ),
        out_shape=[shape, shape],
        compiler_params=pltpu.CompilerParams(vmem_limit_bytes=32 * 2**20),
        cost_estimate=brief,
    )(core_index().reshape(1), left, right)


def ffn_out_kernel(cuts, activ_ref, down_ref, *out_refs):
    total = mat_dot(activ_ref[...], down_ref[...]).astype(narrow)
    for (start, count), out_ref in zip(cuts, out_refs):
        out_ref[...] = total[start : start + count]


def ffn_out_parts(activ, down_proj, sizes):
    group, hidden = activ.shape
    model = down_proj.shape[1]
    tile = 256
    cuts, start = [], 0
    for size in sizes:
        cuts.append((start, size))
        start += size
    return pl.pallas_call(
        functools.partial(ffn_out_kernel, cuts),
        grid=(model // tile,),
        in_specs=[
            pl.BlockSpec((group, hidden), lambda i: (0, 0), pipeline_mode=pl.Buffered(1)),
            pl.BlockSpec((hidden, tile), lambda i: (0, i)),
        ],
        out_specs=[pl.BlockSpec((size, tile), lambda i: (0, i)) for size in sizes],
        out_shape=[jax.ShapeDtypeStruct((size, model), narrow) for size in sizes],
        compiler_params=pltpu.CompilerParams(vmem_limit_bytes=32 * 2**20),
        cost_estimate=brief,
    )(activ, down_proj)


def ffn_back_kernel(cuts, gate_grad_ref, up_grad_ref, gate_ref, up_ref, *out_refs):
    total = dot_right_t(gate_grad_ref[...], gate_ref[...]) + dot_right_t(up_grad_ref[...], up_ref[...])
    total = total.astype(narrow)
    for (start, count), out_ref in zip(cuts, out_refs):
        out_ref[...] = total[start : start + count]


def ffn_back_parts(gate_grad, up_grad, gate_proj, up_proj, sizes):
    group, hidden = gate_grad.shape
    model = gate_proj.shape[0]
    tile = 256
    cuts, start = [], 0
    for size in sizes:
        cuts.append((start, size))
        start += size
    return pl.pallas_call(
        functools.partial(ffn_back_kernel, cuts),
        grid=(model // tile,),
        in_specs=[
            pl.BlockSpec((group, hidden), lambda i: (0, 0), pipeline_mode=pl.Buffered(1)),
            pl.BlockSpec((group, hidden), lambda i: (0, 0), pipeline_mode=pl.Buffered(1)),
            pl.BlockSpec((tile, hidden), lambda i: (i, 0)),
            pl.BlockSpec((tile, hidden), lambda i: (i, 0)),
        ],
        out_specs=[pl.BlockSpec((size, tile), lambda i: (0, i)) for size in sizes],
        out_shape=[jax.ShapeDtypeStruct((size, model), narrow) for size in sizes],
        compiler_params=pltpu.CompilerParams(vmem_limit_bytes=40 * 2**20),
        cost_estimate=brief,
    )(gate_grad, up_grad, gate_proj, up_proj)


def project_kernel(low, in_ref, weights_ref, cos_ref, sin_ref, normed_ref, low_ref, packed_ref, attn_ref, ffn_ref, query_ref):
    model = in_ref.shape[1]
    width = low + 2 * HD
    gains = weights_ref[:, width:].astype(wide)
    gains = jnp.sum(gains.reshape(32, model // 32, 128), axis=0)

    def lanes(start, count):
        return jnp.concatenate([gains[k : k + 1] for k in range(start, start + count)], axis=1)

    query_rows, model_rows = low // 128, model // 128
    query_ref[...] = lanes(0, query_rows)
    attn_ref[...] = lanes(query_rows, model_rows)
    ffn_ref[...] = lanes(query_rows + model_rows, model_rows)
    normed = norm_scale(in_ref[...].astype(wide), attn_ref[...]).astype(narrow)
    normed_ref[...] = normed
    low_kv = mat_dot(normed, weights_ref[:, :width])
    low_ref[...] = low_kv[:, :low]
    packed_ref[:, :low] = norm_scale(low_kv[:, :low], query_ref[...]).astype(narrow)
    packed_ref[:, low : low + HD] = turn(low_kv[:, low : low + HD], cos_ref[...], sin_ref[...]).astype(narrow)
    packed_ref[:, low + HD :] = low_kv[:, low + HD :].astype(narrow)


def project_all(block_in, weights, cosine, sine, low):
    rows, model = block_in.shape
    return pl.pallas_call(
        functools.partial(project_kernel, low),
        out_shape=[
            jax.ShapeDtypeStruct((rows, model), narrow),
            jax.ShapeDtypeStruct((rows, low), wide),
            jax.ShapeDtypeStruct((rows, low + 2 * HD), narrow),
            jax.ShapeDtypeStruct((1, model), wide),
            jax.ShapeDtypeStruct((1, model), wide),
            jax.ShapeDtypeStruct((1, low), wide),
        ],
        compiler_params=pltpu.CompilerParams(vmem_limit_bytes=40 * 2**20),
        cost_estimate=brief,
    )(block_in, weights, cosine, sine)


def low_kernel(low_width, p_ref, px_ref, py_ref, low_ref, gain_ref, cos_ref, sin_ref, weights_ref, in_ref, attn_gain_ref,
               hidden_ref, grads_ref, input_ref, attn_ref, query_ref):
    back = p_ref[...].astype(wide) + px_ref[...].astype(wide) + py_ref[...].astype(wide)
    rows_part, terms = norm_back(low_ref[...], gain_ref[...], back[:, :low_width])
    query_ref[...] = jnp.broadcast_to(jnp.sum(terms, axis=0, keepdims=True), query_ref.shape)
    key_part = turn(back[:, low_width : low_width + HD], cos_ref[...], -sin_ref[...])
    grads = jnp.concatenate([rows_part, key_part, back[:, low_width + HD :]], axis=1).astype(narrow)
    grads_ref[...] = grads
    normed_grad = dot_right_t(grads, weights_ref[:, : low_width + 2 * HD])
    rows_part, terms = norm_back(in_ref[...].astype(wide), attn_gain_ref[...], normed_grad)
    attn_ref[...] = jnp.broadcast_to(jnp.sum(terms, axis=0, keepdims=True), attn_ref.shape)
    input_ref[...] = (hidden_ref[...] + rows_part).astype(narrow)


def low_back(parts, query_low, gain_query, cosine, sine, weights, block_in, gain_attn, hidden_grad):
    rows, low = query_low.shape
    model = block_in.shape[1]
    return pl.pallas_call(
        functools.partial(low_kernel, low),
        out_shape=[
            jax.ShapeDtypeStruct((rows, low + 2 * HD), narrow),
            jax.ShapeDtypeStruct((rows, model), narrow),
            jax.ShapeDtypeStruct((8, model), wide),
            jax.ShapeDtypeStruct((8, low), wide),
        ],
        compiler_params=pltpu.CompilerParams(vmem_limit_bytes=40 * 2**20),
        cost_estimate=brief,
    )(*parts, query_low, gain_query, cosine, sine, weights, block_in, gain_attn, hidden_grad)


def low_weight_kernel(low_width, core_ref, normed_ref, grads_ref, gains_ref, give_ref, keep_ref):
    step = pl.program_id(0)
    product = dot_left_t(normed_ref[...], grads_ref[...]).astype(narrow)

    @pl.when(step < 4)
    def _():
        give_ref[:, :low_width] = product
        give_ref[:, low_width:] = gains_ref[...]

    @pl.when(step >= 4)
    def _():
        keep_ref[:, :low_width] = product
        keep_ref[:, low_width:] = gains_ref[...]


def low_weight_grads(normed, grads, gains):
    rows, model = normed.shape
    width = grads.shape[1]
    tile = model // 8
    block = lambda i, core: (core[0] ^ jnp.where(i < 4, 1, 0)) * 4 + lax.rem(i, 4)
    shape = jax.ShapeDtypeStruct((model // 2, width + 128), narrow)
    return pl.pallas_call(
        functools.partial(low_weight_kernel, width),
        grid_spec=pltpu.PrefetchScalarGridSpec(
            num_scalar_prefetch=1,
            grid=(8,),
            in_specs=[
                pl.BlockSpec((rows, tile), lambda i, core: (0, block(i, core))),
                pl.BlockSpec((rows, width), lambda i, core: (0, 0)),
                pl.BlockSpec((tile, 128), lambda i, core: (block(i, core), 0)),
            ],
            out_specs=[
                pl.BlockSpec((tile, width + 128), lambda i, core: (jnp.minimum(i, 3), 0)),
                pl.BlockSpec((tile, width + 128), lambda i, core: (jnp.maximum(i - 4, 0), 0)),
            ],
        ),
        out_shape=[shape, shape],
        compiler_params=pltpu.CompilerParams(vmem_limit_bytes=32 * 2**20),
        cost_estimate=brief,
    )(core_index().reshape(1), normed, grads, gains)


def spread_kernel(keep_ref, got_ref, own_ref, x_ref, y_ref, far_x_ref, far_y_ref):
    me = lax.axis_index("mp")
    rows = own_ref.shape[0]
    for r, out_refs in enumerate(((own_ref,), (x_ref,), (y_ref,), (far_x_ref, far_y_ref))):
        start = pl.multiple_of((me ^ r) * rows, rows)
        for k, out_ref in enumerate(out_refs):
            size = out_ref.shape[0]
            at = pl.ds(start + k * size, size)
            out_ref[...] = (keep_ref[at].astype(wide) + got_ref[at].astype(wide)).astype(narrow)


def spread_sum(keep, got):
    rows, columns = keep.shape[0] // 4, keep.shape[1]
    return pl.pallas_call(
        spread_kernel,
        out_shape=[
            jax.ShapeDtypeStruct((size, columns), narrow) for size in (rows, rows, rows, rows // 2, rows // 2)
        ],
        compiler_params=pltpu.CompilerParams(vmem_limit_bytes=32 * 2**20),
        cost_estimate=brief,
    )(keep, got)


def body(
    block_in,
    query_down,
    query_up,
    key_proj,
    value_proj,
    out_proj,
    gate_proj,
    up_proj,
    down_proj,
    attn_gain,
    query_gain,
    ffn_gain,
    seq_lens,
    seq_starts,
    out_grad,
):
    rows, model = block_in.shape
    n_dp, n_mp = lax.axis_size("dp"), lax.axis_size("mp")
    me, dp = lax.axis_index("mp"), lax.axis_index("dp")
    group = rows * n_mp
    low = query_down.shape[1]
    share = query_down.shape[0]
    small = on_small_mesh()

    first = [query_down, key_proj, value_proj]
    if small:
        device = dp * n_mp + me
        gains, start = jnp.zeros((share * 128,), narrow), 0
        for gain in (query_gain, attn_gain, ffn_gain):
            gains = lax.dynamic_update_slice_in_dim(gains, gain, start + device * gain.shape[0], 0)
            start += gain.shape[0] * n_dp * n_mp
        first.append(gains.reshape(share, 128))
    first = jnp.concatenate(first, axis=1)
    slot_ids = jnp.arange(group, dtype=jnp.int32)
    width = query_up.shape[1] // n_mp

    def tables(*earlier):
        slots = after(slot_ids, *earlier) if earlier else slot_ids
        segment, position = slot_layout(seq_lens[0], seq_starts[0], slots)
        cosine, sine = rope_tables(position)
        return segment, cosine, sine, [
            lax.dynamic_slice_in_dim(table, me * rows, rows, 0) for table in (cosine, sine)
        ]

    if small:
        line_pairs, line_back = [(0, 1), (1, 2), (2, 3)], [(1, 0), (2, 1), (3, 2)]
        u1, d1 = z_move(first, line_pairs), z_move(first, line_back)
        half = rows // 2
        cot_halves = [out_grad[:half], out_grad[half:]]
        cot_x0, cot_y0 = swap_mp(cot_halves[0], 1), swap_mp(cot_halves[0], 2)
        cuts = [lax.dynamic_slice_in_dim(query_up, (me ^ r) * width, width, 1) for r in range(4)]
        plane = [cuts[0]] + [swap_mp(cuts[r], r) for r in range(1, 4)]
        u2, d2 = z_move(u1, line_pairs[1:]), z_move(d1, line_back[:2])
        u3, d3 = z_move(u2, line_pairs[2:]), z_move(d2, line_back[:1])
        near = [u3, u2, u1, first, d1, d2, d3]
        z = z_index()
        own = jnp.stack([choose(z, [near[3 + j - k] for k in range(4)]) for j in range(4)])
        own, cot_x0, cot_y0 = lax.optimization_barrier((own, cot_x0, cot_y0))
        own_x, own_y = swap_mp(own, 1), swap_mp(own, 2)
        late = jnp.concatenate([jnp.concatenate(plane, axis=0), out_proj], axis=1)
        late = after(late, own)
        u1, d1 = z_move(late, line_pairs), z_move(late, line_back)
        segment, cosine, sine, (own_cos, own_sin) = tables(own)
        flow = Flow(cosine[:8])
        own, own_x, own_y = flow.put(own, own_x, own_y)
        far_x, far_y = swap_mp(own_y[:2], 1), swap_mp(own_x[2:], 2)
        others = [swap_core(piece) for piece in (own, own_x, own_y)]
        u1, d1 = flow.put(u1, d1)
        u2, d2 = z_move(u1, line_pairs[1:]), z_move(d1, line_back[:2])
        far_x, far_y, *others = flow.put(far_x, far_y, *others)
        others += [swap_core(far_x), swap_core(far_y)]
        cot_half = flow.take(cot_halves[1])
        cot_x1, cot_y1 = swap_mp(cot_half, 1), swap_mp(cot_half, 2)
        cot_far_x = swap_mp(cot_y0, 1)
        weights = flow.put(assemble_rows([own, own_x, own_y, far_x, far_y], others, *first.shape)).reshape(model, -1)
        normed, query_low, packed_own, gain_attn, gain_ffn, gain_query = flow.put(
            *project_all(block_in, weights, own_cos, own_sin, low)
        )
        cot_x1, cot_y1, cot_far_x = flow.put(cot_x1, cot_y1, cot_far_x)
        packed_x, packed_y = swap_mp(packed_own, 1), swap_mp(packed_own, 2)
        u2, d2 = flow.put(u2, d2)
        u3, d3 = z_move(u2, line_pairs[2:]), z_move(d2, line_back[:1])

        def by_owner(v):
            return v.reshape(-1, 4, 8, share).swapaxes(1, 2).reshape(-1, model)

        normed_owner = flow.put(by_owner(normed))
        packed_x, packed_y = flow.put(packed_x, packed_y)
        packed_far = swap_mp(packed_y[:half], 1), swap_mp(packed_x[half:], 2)
        cot_far_y = swap_mp(flow.take(cot_x1), 2)
        u3, d3 = flow.put(u3, d3)
        up_line, out_line = flow.put(*order_line([u3, u2, u1, late, d1, d2, d3], width))
        up_other = swap_core(up_line)
        packed_far = flow.put(*packed_far)
        out_cuts = flow.take(*[out_line[r] for r in range(4)])
        mine = [out_cuts[0]] + [swap_mp(out_cuts[r], r) for r in range(1, 4)]
        up_own = flow.put(assemble_up(up_line, up_other, query_up.shape[0], width)).reshape(-1, width)
        packed = flow.put(stack_rows([packed_own, packed_x, packed_y, *packed_far]))
        cot_far_y = flow.put(cot_far_y)
        cot_parts = [out_grad, cot_x0, cot_x1, cot_y0, cot_y1, cot_far_x, cot_far_y]
    else:
        segment, cosine, sine, (own_cos, own_sin) = tables()
        weights = lax.all_gather(first, ("dp", "mp"), axis=0, tiled=True)
        up_all = lax.all_gather(query_up, ("dp", "mp"), axis=0, tiled=True)
        out_all = lax.all_gather(out_proj, ("dp", "mp"), axis=0, tiled=True)
        up_own = lax.dynamic_slice_in_dim(up_all, me * width, width, 1)
        out_own = lax.dynamic_slice_in_dim(out_all, me * width, width, 0)
        cot_rows = mp_gather(out_grad).reshape(group, model)
        gain_attn, gain_query, gain_ffn = (
            lax.all_gather(gain, ("dp", "mp"), axis=0, tiled=True).astype(wide)[None]
            for gain in (attn_gain, query_gain, ffn_gain)
        )
        normed = norm_scale(block_in.astype(wide), gain_attn).astype(narrow)
        low_kv = mat_dot(normed, weights)
        query_low = low_kv[:, :low]
        packed_own = jnp.concatenate(
            [
                norm_scale(query_low, gain_query).astype(narrow),
                turn(low_kv[:, low : low + HD], own_cos, own_sin).astype(narrow),
                low_kv[:, low + HD :].astype(narrow),
            ],
            axis=1,
        )
        packed = mp_gather(packed_own).reshape(group, -1)
    block_rows = block_in.astype(wide)
    sizes = [rows] * 3 + [rows // 2] * 2 if small else [rows] * n_mp
    rotated, mixed, stats = attend(packed, up_own, cosine, sine, segment, rows)
    if small:
        rotated, mixed = flow.put(rotated, mixed)
        mine = flow.put(*mine)
        out_own = flow.put(assemble_out(mine, [swap_core(piece) for piece in mine])).reshape(-1, model)
        cot_rows = stack_rows(cot_parts)
        hidden_sum = MpSum(flow.put(*ffn_out_parts(flow.take(mixed), out_own, sizes)))
        hidden_sum.from_x, hidden_sum.from_y = flow.put(hidden_sum.from_x, hidden_sum.from_y)
        hidden_sum.middle()
        hidden_sum.got = flow.put(*hidden_sum.got)
        hidden_one = block_rows + hidden_sum.end()
        ffn_in = flow.put(norm_scale(hidden_one, gain_ffn).astype(narrow))
        ffn_x, ffn_y = flow.put(swap_mp(ffn_in, 1), swap_mp(ffn_in, 2))
        ffn_far = flow.put(swap_mp(ffn_y[:half], 1), swap_mp(ffn_x[half:], 2))
        ffn_rows = flow.put(stack_rows([ffn_in, ffn_x, ffn_y, *ffn_far]))
    else:
        hidden_one = block_rows + mp_scatter_sum(ffn_out_parts(mixed, out_own, sizes))
        ffn_in = norm_scale(hidden_one, gain_ffn).astype(narrow)
        ffn_rows = mp_gather(ffn_in).reshape(group, model)
    activ, gate_grad, up_grad = ffn(ffn_rows, cot_rows, gate_proj, up_proj, down_proj)
    if not small:
        down_grad = left_t(activ, cot_rows)
        back_parts = ffn_back_parts(gate_grad, up_grad, gate_proj, up_proj, sizes)
        gate_weight_grad = left_t(ffn_rows, gate_grad)
        up_weight_grad = left_t(ffn_rows, up_grad)
        ffn_in_grad = mp_scatter_sum(back_parts)
        hidden_part, ffn_gain_terms = norm_back(hidden_one, gain_ffn, ffn_in_grad)
        hidden_grad = out_grad.astype(wide) + hidden_part
        attn_grad = mp_gather(hidden_grad.astype(narrow)).reshape(group, model)
        turned, *back = attend_back(
            rotated, packed, attn_grad, out_own, up_own, stats, cosine, sine, segment, rows, sizes
        )
        out_part = left_t(attn_grad, mixed)
        up_part = left_t(packed[:, :low], turned)
        own_back = mp_scatter_sum(back)
        block_out = (hidden_one + mp_scatter_sum(ffn_out_parts(activ, down_proj, sizes))).astype(narrow)
    else:
        activ, gate_grad, up_grad = flow.put(activ, gate_grad, up_grad)
        share_d = lax.psum_scatter(flow.put(left_t(activ, cot_rows)), "dp", scatter_dimension=0, tiled=True)
        gate_grad, up_grad = flow.take(gate_grad, up_grad)
        back_sum = MpSum(flow.put(*ffn_back_parts(gate_grad, up_grad, gate_proj, up_proj, sizes)))
        gate_grad, up_grad = flow.take(gate_grad, up_grad)
        weight_pair = flow.put(left_t_pair(ffn_rows, gate_grad, up_grad, n_dp))
        back_sum.from_x, back_sum.from_y = flow.put(back_sum.from_x, back_sum.from_y)
        back_sum.middle()
        out_sizes = ffn_out_parts(flow.take(activ), down_proj, sizes)
        out_sizes = flow.put(*out_sizes)
        back_sum.got = flow.put(*back_sum.got)
        ffn_in_grad = back_sum.end()
        hidden_part, ffn_gain_terms = norm_back(hidden_one, gain_ffn, ffn_in_grad)
        hidden_grad = out_grad.astype(wide) + hidden_part
        attn_own = flow.put(hidden_grad.astype(narrow))
        ffn_gain_sum = jnp.sum(after(ffn_gain_terms, attn_own), axis=0, keepdims=True)
        attn_x, attn_y = swap_mp(attn_own, 1), swap_mp(attn_own, 2)
        share_d, weight_pair = flow.put(share_d, weight_pair)
        share_pair = lax.psum_scatter(weight_pair, "dp", scatter_dimension=0, tiled=True)
        u1, d1 = z_move(share_d, line_pairs), z_move(share_d, line_back)
        attn_x, attn_y = flow.put(attn_x, attn_y)
        attn_far = swap_mp(attn_y[:half], 1), swap_mp(attn_x[half:], 2)
        attn_far = flow.put(*attn_far)
        attn_grad = flow.put(stack_rows([attn_own, attn_x, attn_y, *attn_far]))
        u1, d1 = flow.put(u1, d1)
        u2, d2 = z_move(u1, line_pairs[1:]), z_move(d1, line_back[:2])
        out_sum = MpSum(flow.take(*out_sizes))
        attn_grad = flow.take(attn_grad)
        turned, *back = flow.put(
            *attend_back(rotated, packed, attn_grad, out_own, up_own, stats, cosine, sine, segment, rows, sizes)
        )
        own_sum = MpSum(back)
        give_out, keep_out = flow.put(
            *left_t_halves(flow.take(attn_grad), mixed, model, model // n_dp, by_turns=True)
        )
        got_out = swap_core(give_out)
        own_sum.from_x, own_sum.from_y = flow.put(own_sum.from_x, own_sum.from_y)
        own_sum.middle()
        give_up, keep_up = flow.put(*left_t_halves(packed, flow.take(turned), low, low // n_dp, by_turns=True))
        got_up = swap_core(give_up)
        got_out, got_up = flow.put(got_out, got_up)
        sum_late = flow.put(add_blocks(n_dp // 2, keep_out, got_out, keep_up, got_up))
        z_late = ZSum(lambda k: lax.dynamic_index_in_dim(sum_late, k, 0, keepdims=False))
        own_sum.got = flow.put(*own_sum.got)
        low_grads, input_grad, attn_sum, query_sum = flow.put(
            *low_back(
                [own_sum.parts[0], *own_sum.got],
                query_low,
                gain_query,
                own_cos,
                own_sin,
                weights,
                block_in,
                gain_attn,
                hidden_grad,
            )
        )

        query_sum = jnp.pad(query_sum[:1].reshape(n_dp * n_mp, -1), ((0, 0), (0, share - query_gain.shape[0])))
        gains = by_owner(jnp.concatenate([attn_sum[:1], ffn_gain_sum, query_sum.reshape(1, -1)]))
        gains = jnp.pad(gains.astype(narrow).T, ((0, 0), (0, 125)))
        gains = flow.put(gains)
        give_low, keep_low = flow.put(*low_weight_grads(normed_owner, low_grads, gains))
        got_low = swap_core(give_low)
        keep_low, got_low = flow.put(keep_low, got_low)
        low_sum = MpSum(flow.put(*spread_sum(keep_low, got_low)))
        u2, d2 = flow.put(u2, d2)
        u3, d3 = z_move(u2, line_pairs[2:]), z_move(d2, line_back[:1])
        low_sum.from_x, low_sum.from_y = flow.put(low_sum.from_x, low_sum.from_y)
        low_sum.middle()
        share_pair = flow.put(share_pair)
        pair_sum = lax.all_gather(share_pair, "dp", axis=0, tiled=True)
        z_late.up, z_late.down = flow.put(z_late.up, z_late.down)
        z_late.middle()
        low_sum.got = flow.put(*low_sum.got)
        sum_low = flow.put(low_sum.end().astype(narrow)).reshape(4, share, -1)
        z_low = ZSum(lambda k: lax.dynamic_index_in_dim(sum_low, k, 0, keepdims=False))
        out_sum.from_x, out_sum.from_y = flow.put(out_sum.from_x, out_sum.from_y)
        out_sum.middle()
        z_late.up, z_late.down = flow.put(z_late.up, z_late.down)
        z_late.last()
        z_low.up, z_low.down = flow.put(z_low.up, z_low.down)
        z_low.middle()
        u3, d3 = flow.put(u3, d3)
        own_d = flow.put(in_line([u3, u2, u1, share_d, d1, d2, d3]))
        other_d = swap_core(own_d)
        out_sum.got = flow.put(*out_sum.got)
        block_out = flow.put((hidden_one + out_sum.end()).astype(narrow))
        z_low.up, z_low.down = flow.put(z_low.up, z_low.down)
        z_low.last()
        own_d, other_d = flow.put(own_d, other_d)
        down_proj_grad = flow.put(weave(own_d, other_d))
        z_late.up, z_late.down = flow.put(z_late.up, z_late.down)
        sum_late = z_late.end()
        out_proj_grad = sum_late[: model // n_dp]
        query_up_grad = sum_late[model // n_dp :]
        z_low.up, z_low.down = flow.put(z_low.up, z_low.down)
        pair_sum = flow.put(pair_sum)
        gate_proj_grad, up_proj_grad = flow.put(*widen(pair_sum, n_dp, 2))
        sum_low = z_low.end()
        out_proj_grad = out_proj_grad.astype(wide).T
        sum_low = sum_low + 0.0 * flow.mark[0, 0]
    if not small:
        query_low_part, query_gain_terms = norm_back(query_low, gain_query, own_back[:, :low])
        key_part = turn(own_back[:, low : low + HD], own_cos, -own_sin)
        low_grads = jnp.concatenate([query_low_part, key_part, own_back[:, low + HD :]], axis=1).astype(narrow)
        normed_grad = dot_right_t(low_grads, weights)
        rows_part, attn_gain_terms = norm_back(block_rows, gain_attn, normed_grad)
        input_grad = (hidden_grad + rows_part).astype(narrow)
        gain_parts = [attn_gain_terms.sum(axis=0), ffn_gain_terms.sum(axis=0)]
        query_gain_part = jnp.pad(
            query_gain_terms.sum(axis=0).reshape(n_dp * n_mp, -1), ((0, 0), (0, share - query_gain.shape[0]))
        ).reshape(-1)
        gain_parts = jnp.stack(gain_parts + [query_gain_part])
        out_proj_grad = lax.psum_scatter(out_part, "dp", scatter_dimension=0, tiled=True).astype(wide).T
        query_up_grad = lax.psum_scatter(up_part, "dp", scatter_dimension=0, tiled=True).astype(wide)
        wide_grads = jnp.concatenate(
            [dot_left_t(normed, low_grads), jnp.pad(gain_parts.T, ((0, 0), (0, 125)))], axis=1
        )
        sum_low = lax.psum_scatter(wide_grads, ("dp", "mp"), scatter_dimension=0, tiled=True)
        down_proj_grad = lax.psum(down_grad, "dp").astype(wide)
        gate_proj_grad = lax.psum(gate_weight_grad, "dp").astype(wide)
        up_proj_grad = lax.psum(up_weight_grad, "dp").astype(wide)
    ends = low + 2 * HD
    return (
        block_out,
        input_grad,
        sum_low[:, :low],
        query_up_grad,
        sum_low[:, low : low + HD],
        sum_low[:, low + HD : ends],
        out_proj_grad,
        gate_proj_grad,
        up_proj_grad,
        down_proj_grad,
        sum_low[:, ends],
        sum_low[: query_gain.shape[0], ends + 2],
        sum_low[:, ends + 1],
    )


def solution(mesh):
    both = ("dp", "mp")
    placed = (
        P(both, None),
        P(both, None),
        P(both, None),
        P(both, None),
        P(both, None),
        P(both, None),
        P(None, "mp"),
        P(None, "mp"),
        P("mp", None),
        P(both),
        P(both),
        P(both),
        P("dp", None),
        P("dp", None),
        P(both, None),
    )
    return jax.shard_map(
        body,
        mesh=mesh,
        in_specs=placed,
        out_specs=(
            P(both, None),
            P(both, None),
            P(both, None),
            P("dp", "mp"),
            P(both, None),
            P(both, None),
            P("mp", "dp"),
            P(None, "mp"),
            P(None, "mp"),
            P("mp", None),
            P(both),
            P(both),
            P(both),
        ),
        check_vma=False,
    )
```
